32 devices in a mesh: dp: 16 (over z, x, core), tensor: 2 (over y).
Axes of the slice: x: 2, y: 2, z: 4, core: 2. Of those that a mesh axis runs over, the one named last changes fastest.
Arguments:
- tokens: bfloat16 [6144, 768], P('dp'), may hold values from -6 to 6
- project_weight: bfloat16 [768, 3, 768], P('dp', None, 'tensor'), may hold values from -0.21875 to 0.21875
- project_bias: float32 [2, 768], P(None, 'tensor'), may hold values from -2 to 2
- output_weight: bfloat16 [768, 768], P('tensor', 'dp'), may hold values from -0.875 to 0.875
- output_bias: float32 [2, 768], replicated, may hold values from -2 to 2
- expand_weight: bfloat16 [768, 3072], P('dp', 'tensor'), may hold values from -0.21875 to 0.21875
- expand_bias: float32 [3072], P('tensor'), may hold values from -2 to 2
- shrink_weight: bfloat16 [3072, 768], P('tensor', 'dp'), may hold values from -0.109375 to 0.109375
- norm_gain: float32 [2, 768], replicated, may hold values from 0.5 to 1.5
- norm_shift: float32 [2, 768], replicated, may hold values from -2 to 2
- doc_lengths: int32 [16, 4], P('dp'), may hold values from 1 to 256, 384 in all within a row
- cluster_perm: int32 [16, 12, 384], P('dp', 'tensor'), may hold values from 0 to 383, each once within a row
- masked: int32 [6144], P('dp'), may hold values from 0 to 1, as said below
- out_grad: bfloat16 [6144, 768], P('dp'), may hold values from -6 to 6
Outputs:
- layer_out: bfloat16 [6144, 768], P('dp')
- tokens_grad: float32 [6144, 768], P('dp')
- project_weight_grad: float32 [768, 3, 768], P('dp', None, 'tensor')
- project_bias_grad: float32 [2, 768], P(None, 'tensor')
- output_weight_grad: float32 [768, 768], P('tensor', 'dp')
- output_bias_grad: float32 [2, 768], replicated
- expand_weight_grad: float32 [768, 3072], P('dp', 'tensor')
- expand_bias_grad: float32 [3072], P('tensor')
- shrink_weight_grad: float32 [3072, 768], P('tensor', 'dp')
- norm_gain_grad: float32 [2, 768], replicated
- norm_shift_grad: float32 [2, 768], replicated
The draws below stay inside these ranges and needn't reach their ends.
Inputs may be any that keep to these rules, and one draw needn't show every extreme that they name: `doc_lengths`: row g holds, in order, the lengths of the documents packed into the 384 positions of group g; they sum to 384 and the longest is 256. `cluster_perm`: for each group and head, a permutation of the group's positions. `masked`: 1 marks a position whose output gradient counts, 0 one whose gradient is zero.
All inputs are finite; a program needn't handle non-finite values.
Results may differ from the reference program's by a relative error of at most 0.014.
Values may be sent and summed in bfloat16 or wider, within the bound.
No kernel may reach another device: no remote copies, remote signals or barrier semaphores. Data moves between devices by JAX's collectives and lax.ppermute only.
A program may use at most 128 MiB of HBM per device.

```python
import math
import jax
import jax.numpy as jnp
import numpy as np
from jax import lax

D = 768
HEADS = 12
HEAD = 64
FF = 3072
CLUSTER = 128
DOCS = 4
TOK_DEV = 384
LONGEST = 256
TOKENS = 6144
N_DP = 16


def draw_masked(key, part):
    key = jax.random.fold_in(key, 11)
    level_key, cell_key = jax.random.split(key)
    groups = TOKENS // TOK_DEV
    levels = jax.random.randint(level_key, (groups, 1), 0, 5)
    limits = 2 * 2 ** levels
    cells = jax.random.randint(cell_key, (groups, TOK_DEV), 0, 64)
    return (cells < limits).astype(jnp.int32).reshape(TOKENS)


def spiked(array, stream_key, source, target, blocks, factor):
    def block_of(dim):
        return (jnp.arange(array.shape[dim]) // (array.shape[dim] // blocks)).reshape((-1,) + (1,) * (array.ndim - 1 - dim))

    near = jax.random.permutation(stream_key, blocks)[block_of(target)]
    other_side = (block_of(target) + blocks // 2) % blocks
    return jnp.where((block_of(source) == near) | (block_of(source) == other_side), factor * array, array)


def steps_of(rng, dims, cuts, smallest, high):
    gain = 1.0
    for position, shards_of in cuts:
        draws = jax.random.uniform(jax.random.fold_in(jax.random.fold_in(rng, 6), position), (shards_of,), jnp.float32, smallest / len(cuts), high / len(cuts))
        gain = gain * jnp.repeat(jnp.exp(draws), dims[position] // shards_of).reshape((-1,) + (1,) * (len(dims) - 1 - position))
    return gain


def split_up(amount, total, most, slope):
    loads = [(1 << 20) // math.isqrt(standing ** slope) + 1 for standing in range(2, amount + 1)]
    surplus, counts = total - most - (amount - 1), [1] * (amount - 1)
    while surplus > 0:
        candidates = [i for i in range(amount - 1) if counts[i] < most]
        pool, budget = sum([loads[i] for i in candidates]), surplus
        for i in candidates:
            more = min(most - counts[i], max(1, budget * loads[i] // pool), surplus)
            counts[i] = counts[i] + more
            surplus = surplus - more
    return np.array([most] + counts)


def ragged(stream_key, count, total, reach, slope):
    if count == 2:
        one = jax.random.randint(stream_key, (), max(1, total - reach), min(reach, total - 1) + 1)
        return jnp.stack([one, total - one])
    sizes = jnp.asarray(split_up(count, total, reach, slope), jnp.int32)
    twos = (count - 1) // 2
    donor, receiver = sizes[1:1 + 2 * twos:2], sizes[2:2 + 2 * twos:2]
    room = jnp.minimum(donor - 1, reach - receiver)
    moved = jax.random.randint(jax.random.fold_in(stream_key, 1), (twos,), 0, 1 << 20) % (room + 1)
    sizes = sizes.at[1:1 + 2 * twos:2].set(donor - moved).at[2:2 + 2 * twos:2].set(receiver + moved)
    return sizes[jax.random.permutation(jax.random.fold_in(stream_key, 2), count)]


def normal_values(rng, extent, deviation, reach, cuts=(), held_as=jnp.bfloat16):
    array = deviation * jax.random.normal(rng, extent, jnp.float32)
    if cuts:
        array = array * steps_of(rng, extent, cuts, -0.22, 0.18)
    return jnp.clip(array, -reach, reach).astype(held_as)


def noise_with(key, extent, scale, bound, shards, heavy, kind=jnp.bfloat16):
    drawn = scale * jax.random.normal(key, extent, jnp.float32)
    if shards:
        drawn = drawn * steps_of(key, extent, shards, -0.22, 0.18)
    return jnp.clip(spiked(drawn, jax.random.fold_in(key, 3), *heavy), -bound, bound).astype(kind)


def setup_inputs(seed: int = 0) -> dict:
    seeds = jax.random.split(jax.random.key(seed), 15)
    return {
        "tokens": normal_values(seeds[0], (TOKENS, D), 1.0, 6.0, ((0, 16),)),
        "project_weight": normal_values(seeds[1], (D, 3, D), D ** -0.5, 0.21875, ((0, 16), (2, 2))),
        "project_bias": normal_values(seeds[2], (2, D), 0.3, 2.0, ((1, 2),), jnp.float32),
        "output_weight": normal_values(seeds[3], (D, D), (D // 16) ** -0.5, 0.875, ((0, 2), (1, 16))),
        "output_bias": normal_values(seeds[4], (2, D), 0.3, 2.0, (), jnp.float32),
        "expand_weight": normal_values(seeds[5], (D, FF), D ** -0.5, 0.21875, ((0, 16), (1, 2))),
        "expand_bias": normal_values(seeds[6], (FF,), 0.3, 2.0, ((0, 2),), jnp.float32),
        "shrink_weight": normal_values(seeds[7], (FF, D), FF ** -0.5, 0.109375, ((0, 2), (1, 16))),
        "norm_gain": jnp.clip(1.0 + 0.1 * jax.random.normal(seeds[8], (2, D), jnp.float32), 0.5, 1.5),
        "norm_shift": normal_values(seeds[9], (2, D), 0.3, 2.0, (), jnp.float32),
        "doc_lengths": jax.vmap(lambda own: ragged(own, DOCS, TOK_DEV, LONGEST, 2))(jax.random.split(seeds[10], N_DP)).reshape((N_DP, DOCS)).astype(jnp.int32),
        "cluster_perm": jax.vmap(lambda own: jax.random.permutation(own, TOK_DEV))(jax.random.split(seeds[11], N_DP * HEADS)).reshape((N_DP, HEADS, TOK_DEV)).astype(jnp.int32),
        "masked": draw_masked(jax.random.fold_in(seeds[14], 71), 0),
        "out_grad": noise_with(seeds[13], (TOKENS, D), 1.0, 6.0, ((0, 16),), (0, 1, 16, 2.0)),
    }


@jax.custom_vjp
def low(v):
    return lax.optimization_barrier(v.astype(jnp.bfloat16)).astype(jnp.float32)

@jax.custom_vjp
def low_back(v):
    return v

def low_keep(v):
    return (low(v), None)

def low_pass(kept, grad):
    return (grad,)

def back_keep(v):
    return (v, None)

def back_low(kept, grad):
    return (low(grad),)
low.defvjp(low_keep, low_pass)
low_back.defvjp(back_keep, back_low)
norm_eps = 1e-05
highest = lax.Precision.HIGHEST

def layer_norm(rows_in, gain_row, shift_row):
    center = lax.optimization_barrier(jnp.mean(rows_in, axis=-1, keepdims=True))
    offset = rows_in - center
    spread = lax.optimization_barrier(jnp.mean(offset * offset, axis=-1, keepdims=True))
    return offset * lax.rsqrt(spread + norm_eps) * gain_row + shift_row

def doc_index(lengths, row_count):
    bounds = jnp.cumsum(lengths).astype(jnp.int32)
    places = jnp.arange(row_count, dtype=jnp.int32)
    return lax.optimization_barrier(jnp.sum((places[:, None] >= bounds[None, :]).astype(jnp.int32), axis=1))

def group_forward(params, rows_in, perm_rows, lengths):
    project_weight, project_bias, output_weight, output_bias, expand_weight, expand_bias, shrink_weight, norm_gain, norm_shift = params
    row_count = rows_in.shape[0]
    heads_all = project_weight.shape[2] // HEAD
    clusters_all = row_count // CLUSTER
    projected = jnp.einsum('td,dcf->tcf', rows_in, project_weight, precision=highest)
    queries = low_back(low(projected[:, 0] + project_bias[0]))
    keys_all = low_back(low(projected[:, 1]))
    values = low_back(low(projected[:, 2] + project_bias[1]))
    doc_ids = doc_index(lengths, row_count)
    head_rows = jnp.arange(heads_all, dtype=jnp.int32)[:, None]

    def to_clusters(matrix):
        by_head = matrix.reshape(row_count, heads_all, HEAD).transpose(1, 0, 2)
        picked = jnp.take_along_axis(by_head, perm_rows[:, :, None], axis=1)
        return picked.reshape(heads_all, clusters_all, CLUSTER, HEAD)
    q_clusters = to_clusters(queries)
    k_clusters = to_clusters(keys_all)
    v_clusters = to_clusters(values)
    doc_perm = doc_ids[perm_rows].reshape(heads_all, clusters_all, CLUSTER)
    same_doc = doc_perm[..., :, None] == doc_perm[..., None, :]
    raw_scores = jnp.einsum('hcqe,hcke->hcqk', q_clusters, k_clusters, precision=highest) * HEAD ** (-0.5)
    scores = jnp.where(same_doc, low_back(raw_scores), -1e+30)
    row_top = lax.optimization_barrier(jnp.max(scores, axis=-1, keepdims=True))
    exp_terms = jnp.exp(scores - row_top)
    prob_low = low(exp_terms / lax.optimization_barrier(jnp.sum(exp_terms, axis=-1, keepdims=True)))
    mixed_rows = jnp.einsum('hcqk,hcke->hcqe', prob_low, v_clusters, precision=highest)
    mixed_rows = mixed_rows.reshape(heads_all, row_count, HEAD)
    placed = jnp.zeros_like(mixed_rows).at[head_rows, perm_rows].set(mixed_rows)
    attended = low_back(low(placed.transpose(1, 0, 2).reshape(row_count, heads_all * HEAD)))
    attention = low_back(jnp.dot(attended, output_weight, precision=highest)) + output_bias[0]
    first_norm = layer_norm(rows_in + attention, norm_gain[0], norm_shift[0])
    inner_pre = low_back(jnp.dot(low(first_norm), expand_weight, precision=highest) + expand_bias)
    active_low = low(jax.nn.gelu(inner_pre, approximate=False))
    feed_out = low_back(jnp.dot(active_low, shrink_weight, precision=highest)) + output_bias[1]
    return layer_norm(first_norm + feed_out, norm_gain[1], norm_shift[1])

def reference(tokens, project_weight, project_bias, output_weight, output_bias, expand_weight, expand_bias, shrink_weight, norm_gain, norm_shift, doc_lengths, cluster_perm, masked, out_grad):
    params = (project_weight.astype(jnp.float32), project_bias.astype(jnp.float32), output_weight.astype(jnp.float32), output_bias.astype(jnp.float32), expand_weight.astype(jnp.float32), expand_bias.astype(jnp.float32), shrink_weight.astype(jnp.float32), norm_gain.astype(jnp.float32), norm_shift.astype(jnp.float32))
    groups = doc_lengths.shape[0]
    rows_all = tokens.astype(jnp.float32).reshape(groups, TOK_DEV, D)
    cotangent = out_grad.astype(jnp.float32) * masked.astype(jnp.float32)[:, None]
    cotangent = cotangent.reshape(groups, TOK_DEV, D)

    def one_group(totals, pieces):
        rows_in, perm_rows, lengths, seed_grad = pieces

        def forward(weights, rows_now):
            return group_forward(weights, rows_now, perm_rows, lengths)
        result, pull_back = jax.vjp(forward, params, rows_in)
        weight_grads, rows_grad = pull_back(seed_grad)
        totals = jax.tree.map(jnp.add, totals, weight_grads)
        return (totals, (result, rows_grad))
    zero_grads = jax.tree.map(jnp.zeros_like, params)
    totals, outputs = lax.scan(one_group, zero_grads, (rows_all, cluster_perm, doc_lengths, cotangent))
    results, rows_grads = outputs
    project_weight_grad, project_bias_grad, output_weight_grad, output_bias_grad, expand_weight_grad, expand_bias_grad, shrink_weight_grad, norm_gain_grad, norm_shift_grad = totals
    return (results.reshape(TOKENS, D).astype(jnp.bfloat16), rows_grads.reshape(TOKENS, D), project_weight_grad, project_bias_grad, output_weight_grad, output_bias_grad, expand_weight_grad, expand_bias_grad, shrink_weight_grad, norm_gain_grad, norm_shift_grad)
```

```python
import functools

import jax
import jax.numpy as jnp
from jax import lax
from jax.experimental import pallas as pl
from jax.experimental.pallas import tpu as pltpu
from jax.sharding import PartitionSpec as P

HEAD = 64
CLUSTER = 128
PAIR = 128
NORM_EPS = 1e-05
EXCLUDED = -1e30
VMEM_BYTES = 50 * 1024 * 1024

F32 = jnp.float32
BF16 = jnp.bfloat16

NN = (((1,), (0,)), ((), ()))
NT = (((1,), (1,)), ((), ()))
TN = (((0,), (0,)), ((), ()))


def dot(a, b, dims=NN):
    return lax.dot_general(a, b, dims, preferred_element_type=F32)


def swap(array, axis, offset, size):
    return lax.ppermute(array, axis, [(i, i ^ offset) for i in range(size)])


def gather_pieces(shard, dp):
    pieces = {0: shard}
    for base in range(4, dp, 4):
        pieces[base] = swap(shard, "dp", base, dp)
    for offset in sorted(pieces):
        pieces[offset ^ 2] = swap(pieces[offset], "dp", 2, dp)
    for offset in sorted(pieces):
        pieces[offset ^ 1] = swap(pieces[offset], "dp", 1, dp)
    return [pieces[o] for o in range(dp)]


def scatter_sum(keep, send, dp):
    quarter = dp // 4
    got = swap(send, "dp", 1, dp)
    total = keep.astype(F32) + got.astype(F32)
    got = swap(total[quarter:].astype(BF16), "dp", 2, dp)
    total = total[:quarter] + got.astype(F32)
    out = total[0]
    for k in range(1, quarter):
        out = out + swap(total[k].astype(BF16), "dp", 4 * k, dp).astype(F32)
    return out


def sum_all(vector, dp):
    offset = 1
    while offset < dp:
        vector = vector + swap(vector, "dp", offset, dp)
        offset *= 2
    return vector


def other_half(array):
    return lax.ppermute(array, "tensor", [(0, 1), (1, 0)])


def any_spec():
    return pl.BlockSpec(memory_space=pl.ANY)


def vmem_spec():
    return pl.BlockSpec(memory_space=pltpu.VMEM)


def smem_spec():
    return pl.BlockSpec(memory_space=pltpu.SMEM)


def call(body, outs, ins, name, scratch=(), flops=0, nbytes=0, in_specs=None):
    if in_specs is None:
        in_specs = [vmem_spec()] * len(ins)
    return pl.pallas_call(
        body,
        out_shape=tuple(jax.ShapeDtypeStruct(s, d) for s, d in outs),
        in_specs=in_specs,
        out_specs=tuple(vmem_spec() for _ in outs),
        scratch_shapes=list(scratch),
        compiler_params=pltpu.CompilerParams(vmem_limit_bytes=VMEM_BYTES),
        cost_estimate=pl.CostEstimate(flops=flops, bytes_accessed=nbytes, transcendentals=0),
        name=name,
    )(*ins)


def fetch(pieces, whole, sems):
    count = len(pieces)
    copies = []
    me = lax.axis_index("dp") if count > 1 else 0
    for o, piece in enumerate(pieces):
        rows = piece.shape[-2]
        start = pl.multiple_of((me ^ o) * rows, 16) if count > 1 else 0
        if len(piece.shape) == 3:
            target = whole.at[:, pl.ds(start, rows), :]
        else:
            target = whole.at[pl.ds(start, rows), :]
        copy = pltpu.make_async_copy(piece, target, sems.at[o])
        copy.start()
        copies.append(copy)
    return copies


def arrive(copies):
    for copy in copies:
        copy.wait()


def norm_rows(v):
    center = jnp.mean(v, axis=-1, keepdims=True)
    offset = v - center
    spread = jnp.mean(offset * offset, axis=-1, keepdims=True)
    scale = lax.rsqrt(spread + NORM_EPS)
    return offset * scale, scale


def norm_back(e, n, scale, gain):
    ea = e * gain
    return scale * (
        ea
        - jnp.mean(ea, axis=-1, keepdims=True)
        - n * jnp.mean(ea * n, axis=-1, keepdims=True)
    )


def admitted_kernel(heads, docs, lengths_ref, perm_ref, bias_ref):
    rows = bias_ref.shape[1]
    spot = lax.broadcasted_iota(jnp.int32, (rows, PAIR), 0)
    lane = lax.broadcasted_iota(jnp.int32, (rows, PAIR), 1)
    doc = jnp.zeros((rows, PAIR), jnp.int32)
    bound = jnp.int32(0)
    for k in range(docs):
        bound = bound + lengths_ref[0, k]
        doc = doc + (spot >= bound).astype(jnp.int32)
    doc_hot = (lane == doc + PAIR // 2).astype(F32)
    cluster_hot = (lane == spot // CLUSTER).astype(BF16)
    place = lax.broadcasted_iota(jnp.int32, (rows, rows), 0)
    for h in range(heads):
        here = (place == perm_ref[h : h + 1, :]).astype(BF16)
        key = (dot(here, cluster_hot) + doc_hot).astype(BF16)
        same = dot(key, key, NT)
        bias_ref[h] = jnp.where(same > 1.5, 0.0, EXCLUDED).astype(BF16)


def attention_kernel(count, heads, scale, *refs):
    pieces, refs = refs[:count], refs[count:]
    tokens_ref, bias_ref, admit_ref, qkv_ref, prob_ref, out_ref, whole, sems = refs
    arrive(fetch(pieces, whole, sems))
    tokens = tokens_ref[...]
    for s in range(3):
        part = dot(tokens, whole[s])
        if s == 0:
            part = part + bias_ref[0:1, :]
        if s == 2:
            part = part + bias_ref[1:2, :]
        qkv_ref[s] = part.astype(BF16)
    lane = lax.broadcasted_iota(jnp.int32, (tokens.shape[0], PAIR), 1)
    for pair in range(heads // 2):
        columns = slice(pair * PAIR, (pair + 1) * PAIR)
        q = qkv_ref[0, :, columns]
        k = qkv_ref[1, :, columns]
        v = qkv_ref[2, :, columns]
        mixed = []
        for side in range(2):
            mine = (lane < HEAD) if side == 0 else (lane >= HEAD)
            scores = dot(jnp.where(mine, q, jnp.zeros_like(q)), k, NT) * scale
            scores = scores + admit_ref[2 * pair + side].astype(F32)
            top = jnp.max(scores, axis=-1, keepdims=True)
            terms = jnp.exp(scores - top)
            total = jnp.sum(terms, axis=-1, keepdims=True)
            prob = (terms * (1.0 / total)).astype(BF16)
            prob_ref[2 * pair + side] = prob
            mixed.append(dot(prob, v))
        out_ref[:, columns] = jnp.where(lane < HEAD, mixed[0], mixed[1]).astype(BF16)


def output_kernel(count, *refs):
    pieces, refs = refs[:count], refs[count:]
    attended_ref, out_ref, whole, sems = refs
    arrive(fetch(pieces, whole, sems))
    out_ref[...] = dot(attended_ref[...], whole[...], NT).astype(BF16)


def feed_kernel(count, *refs):
    expand, shrink, refs = refs[:count], refs[count : 2 * count], refs[2 * count :]
    (tokens_ref, own_ref, got_ref, out_bias_ref, gain_ref, shift_ref, bias_ref,
     n_ref, scale_ref, low_ref, active_ref, slope_ref, out_ref,
     expand_all, shrink_all, sems) = refs
    one = fetch(expand, expand_all, sems.at[0])
    two = fetch(shrink, shrink_all, sems.at[1])
    attention = own_ref[...].astype(F32) + got_ref[...].astype(F32) + out_bias_ref[0:1, :]
    n, scale = norm_rows(tokens_ref[...].astype(F32) + attention)
    n_ref[...] = n
    scale_ref[...] = jnp.broadcast_to(scale, scale_ref.shape)
    low_ref[...] = (n * gain_ref[0:1, :] + shift_ref[0:1, :]).astype(BF16)
    arrive(one)
    units = expand_all.shape[1]
    step = 256
    for start in range(0, units, step):
        part = slice(start, start + step)
        pre = dot(low_ref[...], expand_all[:, part]) + bias_ref[:, part]
        half = 0.5 * (1.0 + lax.erf(pre * (2.0**-0.5)))
        active_ref[:, part] = (pre * half).astype(BF16)
        bell = jnp.exp(-0.5 * pre * pre) * 0.3989422804014327
        slope_ref[:, part] = (half + pre * bell).astype(BF16)
    arrive(two)
    out_ref[...] = dot(active_ref[...], shrink_all[...], NT).astype(BF16)


def feed_back_kernel(count, *refs):
    expand, shrink, refs = refs[:count], refs[count : 2 * count], refs[2 * count :]
    (n_ref, own_ref, got_ref, out_bias_ref, gain_ref, shift_ref, seed_ref, masked_ref, slope_ref,
     layer_ref, two_ref, low_ref, inner_ref, first_ref, sums_ref, inner_sum_ref,
     expand_all, shrink_all, sems) = refs
    two = fetch(shrink, shrink_all, sems.at[1])
    one = fetch(expand, expand_all, sems.at[0])
    first = n_ref[...] * gain_ref[0:1, :] + shift_ref[0:1, :]
    feed = own_ref[...].astype(F32) + got_ref[...].astype(F32) + out_bias_ref[1:2, :]
    n, scale = norm_rows(first + feed)
    gain = gain_ref[1:2, :]
    layer_ref[...] = (n * gain + shift_ref[1:2, :]).astype(BF16)
    e = seed_ref[...].astype(F32) * masked_ref[...]
    grad = norm_back(e, n, scale, gain)
    two_ref[...] = grad
    low_ref[...] = grad.astype(BF16)
    sums_ref[0:1, :] = jnp.sum(e * n, axis=0, keepdims=True)
    sums_ref[1:2, :] = jnp.sum(e, axis=0, keepdims=True)
    sums_ref[2:3, :] = jnp.sum(grad, axis=0, keepdims=True)
    arrive(two)
    units = shrink_all.shape[1]
    step = 256
    for start in range(0, units, step):
        part = slice(start, start + step)
        inner = (dot(low_ref[...], shrink_all[:, part]) * slope_ref[:, part].astype(F32)).astype(BF16)
        inner_ref[:, part] = inner
        inner_sum_ref[:, part] = jnp.sum(inner.astype(F32), axis=0, keepdims=True)
    arrive(one)
    first_ref[...] = dot(inner_ref[...], expand_all[...], NT).astype(BF16)


def weight_grad_kernel(dp, left_ref, right_ref, keep_ref, send_ref, whole):
    whole[...] = dot(left_ref[...], right_ref[...], TN)
    me = lax.axis_index("dp")
    rows = keep_ref.shape[1]
    for o in range(dp):
        z, x, c = o // 4, (o // 2) % 2, o % 2
        start = pl.multiple_of((me ^ o) * rows, 16)
        block = whole[pl.ds(start, rows), :].astype(BF16)
        target = send_ref if c else keep_ref
        target[x * (dp // 4) + z] = block


def norm_one_back_kernel(own_ref, got_ref, two_ref, n_ref, scale_ref, gain_ref, one_ref, low_ref, sums_ref):
    e = own_ref[...].astype(F32) + got_ref[...].astype(F32) + two_ref[...]
    n = n_ref[...]
    grad = norm_back(e, n, scale_ref[:, 0:1], gain_ref[0:1, :])
    one_ref[...] = grad
    low_ref[...] = grad.astype(BF16)
    sums_ref[0:1, :] = jnp.sum(e * n, axis=0, keepdims=True)
    sums_ref[1:2, :] = jnp.sum(e, axis=0, keepdims=True)
    sums_ref[2:3, :] = jnp.sum(grad, axis=0, keepdims=True)


def attention_back_kernel(count, heads, scale, *refs):
    pieces, refs = refs[:count], refs[count:]
    low_ref, qkv_ref, prob_ref, grads_ref, sums_ref, whole, given, sems = refs
    arrive(fetch(pieces, whole, sems))
    given[...] = dot(low_ref[...], whole[...]).astype(BF16)
    lane = lax.broadcasted_iota(jnp.int32, (given.shape[0], PAIR), 1)
    for pair in range(heads // 2):
        columns = slice(pair * PAIR, (pair + 1) * PAIR)
        q = qkv_ref[0, :, columns]
        k = qkv_ref[1, :, columns]
        v = qkv_ref[2, :, columns]
        d = given[:, columns]
        parts = []
        for side in range(2):
            mine = (lane < HEAD) if side == 0 else (lane >= HEAD)
            prob = prob_ref[2 * pair + side]
            d_prob = dot(jnp.where(mine, d, jnp.zeros_like(d)), v, NT)
            wide = prob.astype(F32)
            center = jnp.sum(d_prob * wide, axis=-1, keepdims=True)
            score = (wide * (d_prob - center)).astype(BF16)
            parts.append((dot(score, k), dot(score, q, TN), dot(prob, d, TN)))
        for s in range(3):
            both = jnp.where(lane < HEAD, parts[0][s], parts[1][s])
            if s < 2:
                both = both * scale
            both = both.astype(BF16)
            grads_ref[s, :, columns] = both
            if s != 1:
                sums_ref[s // 2 : s // 2 + 1, columns] = jnp.sum(both.astype(F32), axis=0, keepdims=True)


def input_grad_kernel(count, *refs):
    pieces, refs = refs[:count], refs[count:]
    grads_ref, out_ref, whole, sems = refs
    arrive(fetch(pieces, whole, sems))
    total = dot(grads_ref[0], whole[0], NT)
    total = total + dot(grads_ref[1], whole[1], NT)
    total = total + dot(grads_ref[2], whole[2], NT)
    out_ref[...] = total.astype(BF16)


def project_grad_kernel(dp, tokens_ref, grads_ref, keep_ref, send_ref, whole):
    me = lax.axis_index("dp")
    rows = keep_ref.shape[2]
    for s in range(3):
        whole[...] = dot(tokens_ref[...], grads_ref[s], TN)
        for o in range(dp):
            z, x, c = o // 4, (o // 2) % 2, o % 2
            start = pl.multiple_of((me ^ o) * rows, 16)
            block = whole[pl.ds(start, rows), :].astype(BF16)
            target = send_ref if c else keep_ref
            target[x * (dp // 4) + z, s] = block


def plain_grad_kernel(left_ref, right_ref, out_ref):
    out_ref[...] = dot(left_ref[...], right_ref[...], TN)


def shards(
    dp,
    tokens,
    project_weight,
    project_bias,
    output_weight,
    output_bias,
    expand_weight,
    expand_bias,
    shrink_weight,
    norm_gain,
    norm_shift,
    doc_lengths,
    cluster_perm,
    masked,
    out_grad,
):
    rows, width = tokens.shape
    piece_rows, _, columns = project_weight.shape
    units = expand_weight.shape[1]
    heads = columns // HEAD
    scale = HEAD ** (-0.5)
    in_pieces = dp >= 4 and dp & (dp - 1) == 0 and piece_rows % 16 == 0

    project_shard = project_weight.transpose(1, 0, 2)
    output_shard = output_weight.T
    shrink_shard = shrink_weight.T
    if in_pieces:
        project_all = gather_pieces(project_shard, dp)
        output_all = gather_pieces(output_shard, dp)
        expand_all = gather_pieces(expand_weight, dp)
        shrink_all = gather_pieces(shrink_shard, dp)
    else:
        project_all = [lax.all_gather(project_shard, "dp", axis=1, tiled=True)]
        output_all = [lax.all_gather(output_shard, "dp", axis=0, tiled=True)]
        expand_all = [lax.all_gather(expand_weight, "dp", axis=0, tiled=True)]
        shrink_all = [lax.all_gather(shrink_shard, "dp", axis=0, tiled=True)]
    count = len(project_all)

    def whole(*shape):
        return pltpu.VMEM(shape, BF16)

    def sems(*shape):
        return pltpu.SemaphoreType.DMA(shape)

    (admit,) = call(
        functools.partial(admitted_kernel, heads, doc_lengths.shape[1]),
        [((heads, rows, rows), BF16)],
        [doc_lengths, cluster_perm[0]],
        "admitted",
        in_specs=[smem_spec(), vmem_spec()],
        flops=2 * heads * rows * rows * 2 * PAIR,
        nbytes=2 * heads * rows * rows,
    )
    qkv, prob, attended = call(
        functools.partial(attention_kernel, count, heads, scale),
        [((3, rows, columns), BF16), ((heads, rows, rows), BF16), ((rows, columns), BF16)],
        [*project_all, tokens, project_bias, admit],
        "attention",
        scratch=[whole(3, width, columns), sems(count)],
        in_specs=[any_spec()] * count + [vmem_spec()] * 3,
        flops=2 * rows * width * 3 * columns + 4 * heads * rows * rows * PAIR,
        nbytes=6 * width * columns,
    )
    (attention_own,) = call(
        functools.partial(output_kernel, count),
        [((rows, width), BF16)],
        [*output_all, attended],
        "attention_output",
        scratch=[whole(width, columns), sems(count)],
        in_specs=[any_spec()] * count + [vmem_spec()],
        flops=2 * rows * width * columns,
        nbytes=2 * width * columns,
    )
    attention_got = other_half(attention_own)
    n_one, scale_one, first_low, active_low, slope, feed_own = call(
        functools.partial(feed_kernel, count),
        [
            ((rows, width), F32),
            ((rows, PAIR), F32),
            ((rows, width), BF16),
            ((rows, units), BF16),
            ((rows, units), BF16),
            ((rows, width), BF16),
        ],
        [
            *expand_all, *shrink_all, tokens, attention_own, attention_got, output_bias,
            norm_gain, norm_shift, expand_bias[None, :],
        ],
        "feed_forward",
        scratch=[whole(width, units), whole(width, units), sems(2, count)],
        in_specs=[any_spec()] * (2 * count) + [vmem_spec()] * 7,
        flops=4 * rows * width * units,
        nbytes=4 * width * units,
    )
    feed_got = other_half(feed_own)
    layer_out, residual_two, feed_low, inner_low, first_own, sums_two, inner_sum = call(
        functools.partial(feed_back_kernel, count),
        [
            ((rows, width), BF16),
            ((rows, width), F32),
            ((rows, width), BF16),
            ((rows, units), BF16),
            ((rows, width), BF16),
            ((3, width), F32),
            ((1, units), F32),
        ],
        [
            *expand_all, *shrink_all, n_one, feed_own, feed_got, output_bias,
            norm_gain, norm_shift, out_grad, masked.astype(F32)[:, None], slope,
        ],
        "feed_backward",
        scratch=[whole(width, units), whole(width, units), sems(2, count)],
        in_specs=[any_spec()] * (2 * count) + [vmem_spec()] * 9,
        flops=4 * rows * width * units,
        nbytes=4 * width * units,
    )
    first_got = other_half(first_own)

    def weight_grad(left, right, name):
        wide = right.shape[1]
        if in_pieces:
            keep, send = call(
                functools.partial(weight_grad_kernel, dp),
                [((dp // 2, piece_rows, wide), BF16)] * 2,
                [left, right],
                name,
                scratch=[pltpu.VMEM((width, wide), F32)],
                flops=2 * rows * width * wide,
                nbytes=2 * width * wide,
            )
            return scatter_sum(keep, send, dp)
        (grad,) = call(plain_grad_kernel, [((width, wide), F32)], [left, right], name)
        return lax.psum_scatter(grad, "dp", scatter_dimension=0, tiled=True)

    shrink_part = weight_grad(feed_low, active_low, "shrink_grad")
    expand_part = weight_grad(first_low, inner_low, "expand_grad")
    residual_one, attention_low, sums_one = call(
        norm_one_back_kernel,
        [((rows, width), F32), ((rows, width), BF16), ((3, width), F32)],
        [first_own, first_got, residual_two, n_one, scale_one, norm_gain],
        "norm_one_backward",
    )
    project_low, project_sums = call(
        functools.partial(attention_back_kernel, count, heads, scale),
        [((3, rows, columns), BF16), ((2, columns), F32)],
        [*output_all, attention_low, qkv, prob],
        "attention_backward",
        scratch=[whole(width, columns), whole(rows, columns), sems(count)],
        in_specs=[any_spec()] * count + [vmem_spec()] * 3,
        flops=2 * rows * width * columns + 8 * heads * rows * rows * PAIR,
        nbytes=2 * width * columns,
    )
    output_part = weight_grad(attention_low, attended, "output_grad")
    (tokens_own,) = call(
        functools.partial(input_grad_kernel, count),
        [((rows, width), BF16)],
        [*project_all, project_low],
        "input_grad",
        scratch=[whole(3, width, columns), sems(count)],
        in_specs=[any_spec()] * count + [vmem_spec()],
        flops=6 * rows * width * columns,
        nbytes=6 * width * columns,
    )
    tokens_got = other_half(tokens_own)
    if in_pieces:
        keep, send = call(
            functools.partial(project_grad_kernel, dp),
            [((dp // 2, 3, piece_rows, columns), BF16)] * 2,
            [tokens, project_low],
            "project_grad",
            scratch=[pltpu.VMEM((width, columns), F32)],
            flops=6 * rows * width * columns,
            nbytes=6 * width * columns,
        )
        project_part = scatter_sum(keep, send, dp)
    else:
        project_part = jnp.stack(
            [weight_grad(tokens, project_low[s], "project_grad") for s in range(3)]
        )
    tokens_grad = tokens_own.astype(F32) + tokens_got.astype(F32) + residual_one

    pieces = [sums_one, sums_two, inner_sum, project_sums]
    vector = jnp.concatenate([p.reshape(-1, PAIR) for p in pieces])
    vector = sum_all(vector, dp) if in_pieces else lax.psum(vector, "dp")
    ends, parts = 0, []
    for p in pieces:
        step = p.size // PAIR
        parts.append(vector[ends : ends + step].reshape(p.shape))
        ends += step
    one, two, inner_total, project_total = parts
    return (
        layer_out,
        tokens_grad,
        project_part.transpose(1, 0, 2),
        project_total,
        output_part.T,
        jnp.stack([one[2], two[2]]),
        expand_part,
        inner_total[0],
        shrink_part.T,
        jnp.stack([one[0], two[0]]),
        jnp.stack([one[1], two[1]]),
    )


def solution(mesh):
    in_specs = (
        P("dp", None),
        P("dp", None, "tensor"),
        P(None, "tensor"),
        P("tensor", "dp"),
        P(),
        P("dp", "tensor"),
        P("tensor"),
        P("tensor", "dp"),
        P(),
        P(),
        P("dp", None),
        P("dp", "tensor", None),
        P("dp"),
        P("dp", None),
    )
    out_specs = (
        P("dp", None),
        P("dp", None),
        P("dp", None, "tensor"),
        P(None, "tensor"),
        P("tensor", "dp"),
        P(),
        P("dp", "tensor"),
        P("tensor"),
        P("tensor", "dp"),
        P(),
        P(),
    )
    body = functools.partial(shards, mesh.shape["dp"])
    return jax.shard_map(body, mesh=mesh, in_specs=in_specs, out_specs=out_specs, check_vma=False)
```

```python
import functools

import jax
import jax.numpy as jnp
from jax import lax
from jax.experimental import pallas as pl
from jax.experimental.pallas import tpu as pltpu
from jax.sharding import PartitionSpec as P

HEAD = 64
CLUSTER = 128
PAIR = 128
NORM_EPS = 1e-05
EXCLUDED = -1e30
VMEM_BYTES = 24 * 1024 * 1024

F32 = jnp.float32
BF16 = jnp.bfloat16

NN = (((1,), (0,)), ((), ()))
NT = (((1,), (1,)), ((), ()))
TN = (((0,), (0,)), ((), ()))


def dot(a, b, dims=NN):
    return lax.dot_general(a, b, dims, preferred_element_type=F32)


def swap(array, axis, offset, size):
    return lax.ppermute(array, axis, [(i, i ^ offset) for i in range(size)])


def after(array, *earlier):
    return lax.optimization_barrier((array, *earlier))[0]


def far_steps(dp):
    steps, step = [], dp // 2
    while step >= 4:
        steps.append(step)
        step //= 2
    return steps


def gather_far(shard, dp, early, late):
    pieces = {0: after(shard, *early) if early else shard}
    for step in far_steps(dp):
        for offset in list(pieces):
            held = after(pieces[offset], *late) if offset and late else pieces[offset]
            pieces[offset ^ step] = swap(held, "dp", step, dp)
    return pieces


def gather_near(pieces, dp, gate):
    pieces = dict(pieces)
    for offset in list(pieces):
        if offset ^ 2 not in pieces:
            held = after(pieces[offset], *gate) if gate else pieces[offset]
            pieces[offset ^ 2] = swap(held, "dp", 2, dp)
    for offset in list(pieces):
        pieces[offset ^ 1] = swap(pieces[offset], "dp", 1, dp)
    return [pieces[o] for o in range(dp)]


def block_orders(dp, steps):
    offsets = [0]
    for step in reversed(steps[1:]):
        offsets = offsets + [o ^ step for o in offsets]
    return offsets, [o ^ steps[0] for o in offsets]


def halve_kernel(*refs):
    (keep_ref, got_ref), outs = refs[:2], refs[2:]
    total = keep_ref[...].astype(F32) + got_ref[...].astype(F32)
    if len(outs) == 1:
        outs[0][...] = total[0]
    else:
        half = total.shape[0] // 2
        outs[0][...] = total[:half]
        outs[1][...] = total[half:].astype(BF16)


def scatter_sum(keep, send, dp, steps, name):
    sends = [send]
    for i, step in enumerate(steps):
        got = swap(send, "dp", step, dp)
        shape = keep.shape[1:]
        half = keep.shape[0] // 2
        last = half == 0
        outs = [(shape, F32)] if last else [((half, *shape), F32), ((half, *shape), BF16)]
        result = call(halve_kernel, outs, [keep, got], f"{name}_sum_{step}")
        if last:
            return result[0], sends
        keep, send = result
        sends.append(send)


def sum_all(vector, dp):
    offset = 1
    while offset < dp:
        vector = vector + swap(vector, "dp", offset, dp)
        offset *= 2
    return vector


def other_half(array):
    return lax.ppermute(array, "tensor", [(0, 1), (1, 0)])


def any_spec():
    return pl.BlockSpec(memory_space=pl.ANY)


def vmem_spec():
    return pl.BlockSpec(memory_space=pltpu.VMEM)


def smem_spec():
    return pl.BlockSpec(memory_space=pltpu.SMEM)


def call(body, outs, ins, name, scratch=(), in_specs=None, us=2):
    if in_specs is None:
        in_specs = [vmem_spec()] * len(ins)
    return pl.pallas_call(
        body,
        out_shape=tuple(jax.ShapeDtypeStruct(s, d) for s, d in outs),
        in_specs=in_specs,
        out_specs=tuple(vmem_spec() for _ in outs),
        scratch_shapes=list(scratch),
        compiler_params=pltpu.CompilerParams(vmem_limit_bytes=VMEM_BYTES),
        cost_estimate=pl.CostEstimate(flops=1000, bytes_accessed=us * 3_000_000, transcendentals=0),
        name=name,
    )(*ins)


def fetch(pieces, whole, sems):
    count = len(pieces)
    copies = []
    me = lax.axis_index("dp") if count > 1 else 0
    for o, piece in enumerate(pieces):
        rows = piece.shape[-2]
        start = pl.multiple_of((me ^ o) * rows, 16) if count > 1 else 0
        if len(piece.shape) == 3:
            target = whole.at[:, pl.ds(start, rows), :]
        else:
            target = whole.at[pl.ds(start, rows), :]
        copy = pltpu.make_async_copy(piece, target, sems.at[o])
        copy.start()
        copies.append(copy)
    return copies


def arrive(copies):
    for copy in copies:
        copy.wait()


def norm_rows(v):
    center = jnp.mean(v, axis=-1, keepdims=True)
    offset = v - center
    spread = jnp.mean(offset * offset, axis=-1, keepdims=True)
    scale = lax.rsqrt(spread + NORM_EPS)
    return offset * scale, scale


def norm_back(e, n, scale, gain):
    ea = e * gain
    return scale * (
        ea
        - jnp.mean(ea, axis=-1, keepdims=True)
        - n * jnp.mean(ea * n, axis=-1, keepdims=True)
    )


def admitted_kernel(heads, docs, lengths_ref, perm_ref, bias_ref):
    rows = bias_ref.shape[1]
    spot = lax.broadcasted_iota(jnp.int32, (rows, PAIR), 0)
    lane = lax.broadcasted_iota(jnp.int32, (rows, PAIR), 1)
    doc = jnp.zeros((rows, PAIR), jnp.int32)
    bound = jnp.int32(0)
    for k in range(docs):
        bound = bound + lengths_ref[0, k]
        doc = doc + (spot >= bound).astype(jnp.int32)
    doc_hot = (lane == doc + PAIR // 2).astype(F32)
    cluster_hot = (lane == spot // CLUSTER).astype(BF16)
    place = lax.broadcasted_iota(jnp.int32, (rows, rows), 0)
    for h in range(heads):
        here = (place == perm_ref[h : h + 1, :]).astype(BF16)
        key = (dot(here, cluster_hot) + doc_hot).astype(BF16)
        same = dot(key, key, NT)
        bias_ref[h] = jnp.where(same > 1.5, 0.0, EXCLUDED).astype(BF16)


def attention_kernel(count, heads, scale, *refs):
    pieces, refs = refs[:count], refs[count:]
    tokens_ref, bias_ref, admit_ref, qkv_ref, prob_ref, attended_ref, out_ref, whole, sems = refs
    arrive(fetch(pieces, whole, sems))
    tokens = tokens_ref[...]
    for s in range(3):
        part = dot(tokens, whole[s])
        if s == 0:
            part = part + bias_ref[0:1, :]
        if s == 2:
            part = part + bias_ref[1:2, :]
        qkv_ref[s] = part.astype(BF16)
    lane = lax.broadcasted_iota(jnp.int32, (tokens.shape[0], PAIR), 1)
    for pair in range(heads // 2):
        columns = slice(pair * PAIR, (pair + 1) * PAIR)
        q = qkv_ref[0, :, columns]
        k = qkv_ref[1, :, columns]
        v = qkv_ref[2, :, columns]
        mixed = []
        for side in range(2):
            mine = (lane < HEAD) if side == 0 else (lane >= HEAD)
            scores = dot(jnp.where(mine, q, jnp.zeros_like(q)), k, NT) * scale
            scores = scores + admit_ref[2 * pair + side].astype(F32)
            top = jnp.max(scores, axis=-1, keepdims=True)
            terms = jnp.exp(scores - top)
            total = jnp.sum(terms, axis=-1, keepdims=True)
            prob = (terms * (1.0 / total)).astype(BF16)
            prob_ref[2 * pair + side] = prob
            mixed.append(dot(prob, v))
        attended_ref[:, columns] = jnp.where(lane < HEAD, mixed[0], mixed[1]).astype(BF16)
    out_ref[...] = dot(attended_ref[...], whole[3], NT).astype(BF16)


def expand_kernel(count, *refs):
    pieces, refs = refs[:count], refs[count:]
    (tokens_ref, own_ref, got_ref, out_bias_ref, gain_ref, shift_ref, bias_ref,
     n_ref, scale_ref, low_ref, active_ref, slope_ref, whole, sems) = refs
    copies = fetch(pieces, whole, sems)
    attention = own_ref[...].astype(F32) + got_ref[...].astype(F32) + out_bias_ref[0:1, :]
    n, scale = norm_rows(tokens_ref[...].astype(F32) + attention)
    n_ref[...] = n
    scale_ref[...] = jnp.broadcast_to(scale, scale_ref.shape)
    low_ref[...] = (n * gain_ref[0:1, :] + shift_ref[0:1, :]).astype(BF16)
    arrive(copies)
    units = whole.shape[1]
    step = 256
    for start in range(0, units, step):
        part = slice(start, start + step)
        pre = dot(low_ref[...], whole[:, part]) + bias_ref[:, part]
        half = 0.5 * (1.0 + lax.erf(pre * (2.0**-0.5)))
        active_ref[:, part] = (pre * half).astype(BF16)
        bell = jnp.exp(-0.5 * pre * pre) * 0.3989422804014327
        slope_ref[:, part] = (half + pre * bell).astype(BF16)


def shrink_kernel(count, *refs):
    pieces, refs = refs[:count], refs[count:]
    active_ref, out_ref, whole, sems = refs
    arrive(fetch(pieces, whole, sems))
    out_ref[...] = dot(active_ref[...], whole[...], NT).astype(BF16)


def feed_back_kernel(
    expand_all, shrink_all, n_ref, own_ref, got_ref, out_bias_ref, gain_ref, shift_ref, seed_ref,
    masked_ref, slope_ref, layer_ref, two_ref, low_ref, inner_ref, first_ref, sums_ref, inner_sum_ref,
):
    first = n_ref[...] * gain_ref[0:1, :] + shift_ref[0:1, :]
    feed = own_ref[...].astype(F32) + got_ref[...].astype(F32) + out_bias_ref[1:2, :]
    n, scale = norm_rows(first + feed)
    gain = gain_ref[1:2, :]
    layer_ref[...] = (n * gain + shift_ref[1:2, :]).astype(BF16)
    e = seed_ref[...].astype(F32) * masked_ref[...]
    grad = norm_back(e, n, scale, gain)
    two_ref[...] = grad
    low_ref[...] = grad.astype(BF16)
    sums_ref[0:1, :] = jnp.sum(e * n, axis=0, keepdims=True)
    sums_ref[1:2, :] = jnp.sum(e, axis=0, keepdims=True)
    sums_ref[2:3, :] = jnp.sum(grad, axis=0, keepdims=True)
    units = shrink_all.shape[1]
    step = 256
    for start in range(0, units, step):
        part = slice(start, start + step)
        inner = (dot(low_ref[...], shrink_all[:, part]) * slope_ref[:, part].astype(F32)).astype(BF16)
        inner_ref[:, part] = inner
        inner_sum_ref[:, part] = jnp.sum(inner.astype(F32), axis=0, keepdims=True)
    first_ref[...] = dot(inner_ref[...], expand_all[...], NT).astype(BF16)


def weight_grad_kernel(orders, left_ref, right_ref, keep_ref, send_ref, whole):
    whole[...] = dot(left_ref[...], right_ref[...], TN)
    me = lax.axis_index("dp")
    rows = keep_ref.shape[1]
    for order, target in zip(orders, (keep_ref, send_ref)):
        for k, o in enumerate(order):
            start = pl.multiple_of((me ^ o) * rows, 16)
            target[k] = whole[pl.ds(start, rows), :].astype(BF16)


def norm_one_back_kernel(own_ref, got_ref, two_ref, n_ref, scale_ref, gain_ref, one_ref, low_ref, sums_ref):
    e = own_ref[...].astype(F32) + got_ref[...].astype(F32) + two_ref[...]
    n = n_ref[...]
    grad = norm_back(e, n, scale_ref[:, 0:1], gain_ref[0:1, :])
    one_ref[...] = grad
    low_ref[...] = grad.astype(BF16)
    sums_ref[0:1, :] = jnp.sum(e * n, axis=0, keepdims=True)
    sums_ref[1:2, :] = jnp.sum(e, axis=0, keepdims=True)
    sums_ref[2:3, :] = jnp.sum(grad, axis=0, keepdims=True)


def attention_back_kernel(heads, scale, whole_ref, low_ref, qkv_ref, prob_ref, grads_ref, sums_ref, given):
    given[...] = dot(low_ref[...], whole_ref[3]).astype(BF16)
    lane = lax.broadcasted_iota(jnp.int32, (given.shape[0], PAIR), 1)
    for pair in range(heads // 2):
        columns = slice(pair * PAIR, (pair + 1) * PAIR)
        q = qkv_ref[0, :, columns]
        k = qkv_ref[1, :, columns]
        v = qkv_ref[2, :, columns]
        d = given[:, columns]
        parts = []
        for side in range(2):
            mine = (lane < HEAD) if side == 0 else (lane >= HEAD)
            prob = prob_ref[2 * pair + side]
            d_prob = dot(jnp.where(mine, d, jnp.zeros_like(d)), v, NT)
            wide = prob.astype(F32)
            center = jnp.sum(d_prob * wide, axis=-1, keepdims=True)
            score = (wide * (d_prob - center)).astype(BF16)
            parts.append((dot(score, k), dot(score, q, TN), dot(prob, d, TN)))
        for s in range(3):
            both = jnp.where(lane < HEAD, parts[0][s], parts[1][s])
            if s < 2:
                both = both * scale
            both = both.astype(BF16)
            grads_ref[s, :, columns] = both
            if s != 1:
                sums_ref[s // 2 : s // 2 + 1, columns] = jnp.sum(both.astype(F32), axis=0, keepdims=True)


def input_grad_kernel(whole_ref, grads_ref, out_ref):
    total = dot(grads_ref[0], whole_ref[0], NT)
    total = total + dot(grads_ref[1], whole_ref[1], NT)
    total = total + dot(grads_ref[2], whole_ref[2], NT)
    out_ref[...] = total.astype(BF16)


def project_grad_kernel(orders, tokens_ref, grads_ref, keep_ref, send_ref, whole):
    me = lax.axis_index("dp")
    rows = keep_ref.shape[2]
    for s in range(3):
        whole[...] = dot(tokens_ref[...], grads_ref[s], TN)
        for order, target in zip(orders, (keep_ref, send_ref)):
            for k, o in enumerate(order):
                start = pl.multiple_of((me ^ o) * rows, 16)
                target[k, s] = whole[pl.ds(start, rows), :].astype(BF16)


def plain_grad_kernel(left_ref, right_ref, out_ref):
    out_ref[...] = dot(left_ref[...], right_ref[...], TN)


def shards(
    dp,
    tokens,
    project_weight,
    project_bias,
    output_weight,
    output_bias,
    expand_weight,
    expand_bias,
    shrink_weight,
    norm_gain,
    norm_shift,
    doc_lengths,
    cluster_perm,
    masked,
    out_grad,
):
    rows, width = tokens.shape
    piece_rows, _, columns = project_weight.shape
    units = expand_weight.shape[1]
    heads = columns // HEAD
    scale = HEAD ** (-0.5)
    in_pieces = dp >= 4 and dp & (dp - 1) == 0 and piece_rows % 16 == 0

    mixer_shard = jnp.concatenate([project_weight.transpose(1, 0, 2), output_weight.T[None]])
    shrink_shard = shrink_weight.T
    (admit,) = call(
        functools.partial(admitted_kernel, heads, doc_lengths.shape[1]),
        [((heads, rows, rows), BF16)],
        [doc_lengths, cluster_perm[0]],
        "admitted",
        in_specs=[smem_spec(), vmem_spec()],
    )
    if in_pieces:
        mixer_first = {2: swap(mixer_shard, "dp", 2, dp)}
        mixer_far = gather_far(mixer_shard, dp, (), (mixer_first[2], admit))
        mixer_all = gather_near({**mixer_far, **mixer_first}, dp, ())
        expand_own = after(expand_weight, mixer_all[10])
        expand_first = {2: swap(after(expand_weight, mixer_all[14]), "dp", 2, dp)}
    else:
        mixer_all = [lax.all_gather(mixer_shard, "dp", axis=1, tiled=True)]
        expand_all = [lax.all_gather(expand_weight, "dp", axis=0, tiled=True)]
        shrink_all = [lax.all_gather(shrink_shard, "dp", axis=0, tiled=True)]
    count = len(mixer_all)

    def whole(*shape):
        return pltpu.VMEM(shape, BF16)

    def sems(*shape):
        return pltpu.SemaphoreType.DMA(shape)

    qkv, prob, attended, attention_own, mixer = call(
        functools.partial(attention_kernel, count, heads, scale),
        [
            ((3, rows, columns), BF16),
            ((heads, rows, rows), BF16),
            ((rows, columns), BF16),
            ((rows, width), BF16),
            ((4, width, columns), BF16),
        ],
        [*mixer_all, tokens, project_bias, admit],
        "attention",
        scratch=[sems(count)],
        in_specs=[any_spec()] * count + [vmem_spec()] * 3,
        us=7,
    )
    attention_got = other_half(attention_own)
    if in_pieces:
        expand_far = gather_far(expand_own, dp, (), (qkv,))
        expand_all = gather_near({**expand_far, **expand_first}, dp, (qkv,))
        ends = (expand_far[max(expand_far)],)
        shrink_far = gather_far(shrink_shard, dp, ends, ())
        shrink_all = gather_near(shrink_far, dp, ends)
    n_one, scale_one, first_low, active_low, slope, expand = call(
        functools.partial(expand_kernel, count),
        [
            ((rows, width), F32),
            ((rows, PAIR), F32),
            ((rows, width), BF16),
            ((rows, units), BF16),
            ((rows, units), BF16),
            ((width, units), BF16),
        ],
        [
            *expand_all, tokens, attention_own, attention_got, output_bias,
            norm_gain, norm_shift, expand_bias[None, :],
        ],
        "expand",
        scratch=[sems(count)],
        in_specs=[any_spec()] * count + [vmem_spec()] * 7,
        us=7,
    )
    feed_own, shrink = call(
        functools.partial(shrink_kernel, count),
        [((rows, width), BF16), ((width, units), BF16)],
        [*shrink_all, active_low],
        "shrink",
        scratch=[sems(count)],
        in_specs=[any_spec()] * count + [vmem_spec()],
    )
    feed_got = other_half(feed_own)
    layer_out, residual_two, feed_low, inner_low, first_own, sums_two, inner_sum = call(
        feed_back_kernel,
        [
            ((rows, width), BF16),
            ((rows, width), F32),
            ((rows, width), BF16),
            ((rows, units), BF16),
            ((rows, width), BF16),
            ((3, width), F32),
            ((1, units), F32),
        ],
        [
            expand, shrink, n_one, feed_own, feed_got, output_bias,
            norm_gain, norm_shift, out_grad, masked.astype(F32)[:, None], slope,
        ],
        "feed_backward",
        us=9,
    )
    first_got = other_half(first_own)

    far = far_steps(dp)[::-1]

    def weight_grad(left, right, name, steps):
        wide = right.shape[1]
        if in_pieces:
            keep, send = call(
                functools.partial(weight_grad_kernel, block_orders(dp, steps)),
                [((dp // 2, piece_rows, wide), BF16)] * 2,
                [left, right],
                name,
                scratch=[pltpu.VMEM((width, wide), F32)],
            )
            total, sends = scatter_sum(keep, send, dp, steps, name)
            return sends, total
        (grad,) = call(plain_grad_kernel, [((width, wide), F32)], [left, right], name)
        return [grad] * 4, lax.psum_scatter(grad, "dp", scatter_dimension=0, tiled=True)

    shrink_sends, shrink_part = weight_grad(feed_low, active_low, "shrink_grad", [1, 2, *far])
    expand_sends, expand_part = weight_grad(
        first_low, after(inner_low, shrink_sends[0]), "expand_grad", [1, 2, *far]
    )
    residual_one, attention_low, sums_one = call(
        norm_one_back_kernel,
        [((rows, width), F32), ((rows, width), BF16), ((3, width), F32)],
        [first_own, first_got, residual_two, n_one, scale_one, after(norm_gain, shrink_sends[1], expand_sends[1])],
        "norm_one_backward",
    )
    output_sends, output_part = weight_grad(attention_low, attended, "output_grad", [1, 2, *far])
    project_low, project_sums = call(
        functools.partial(attention_back_kernel, heads, scale),
        [((3, rows, columns), BF16), ((2, columns), F32)],
        [mixer, after(attention_low, output_sends[1], shrink_sends[2]), qkv, prob],
        "attention_backward",
        scratch=[whole(rows, columns)],
        us=5,
    )
    (tokens_own,) = call(
        input_grad_kernel,
        [((rows, width), BF16)],
        [mixer, project_low],
        "input_grad",
    )
    tokens_got = other_half(tokens_own)
    if in_pieces:
        steps = [1, 2, *far]
        keep, send = call(
            functools.partial(project_grad_kernel, block_orders(dp, steps)),
            [((dp // 2, 3, piece_rows, columns), BF16)] * 2,
            [tokens, project_low],
            "project_grad",
            scratch=[pltpu.VMEM((width, columns), F32)],
        )
        project_part, _ = scatter_sum(keep, send, dp, steps, "project_grad")
    else:
        project_part = jnp.stack(
            [weight_grad(tokens, project_low[s], "project_grad", [])[1] for s in range(3)]
        )
    tokens_grad = tokens_own.astype(F32) + tokens_got.astype(F32) + residual_one

    pieces = [sums_one, sums_two, inner_sum, project_sums]
    vector = jnp.concatenate([p.reshape(-1, PAIR) for p in pieces])
    vector = sum_all(vector, dp) if in_pieces else lax.psum(vector, "dp")
    ends, parts = 0, []
    for p in pieces:
        step = p.size // PAIR
        parts.append(vector[ends : ends + step].reshape(p.shape))
        ends += step
    one, two, inner_total, project_total = parts
    return (
        layer_out,
        tokens_grad,
        project_part.transpose(1, 0, 2),
        project_total,
        output_part.T,
        jnp.stack([one[2], two[2]]),
        expand_part,
        inner_total[0],
        shrink_part.T,
        jnp.stack([one[0], two[0]]),
        jnp.stack([one[1], two[1]]),
    )


def solution(mesh):
    in_specs = (
        P("dp", None),
        P("dp", None, "tensor"),
        P(None, "tensor"),
        P("tensor", "dp"),
        P(),
        P("dp", "tensor"),
        P("tensor"),
        P("tensor", "dp"),
        P(),
        P(),
        P("dp", None),
        P("dp", "tensor", None),
        P("dp"),
        P("dp", None),
    )
    out_specs = (
        P("dp", None),
        P("dp", None),
        P("dp", None, "tensor"),
        P(None, "tensor"),
        P("tensor", "dp"),
        P(),
        P("dp", "tensor"),
        P("tensor"),
        P("tensor", "dp"),
        P(),
        P(),
    )
    body = functools.partial(shards, mesh.shape["dp"])
    return jax.shard_map(body, mesh=mesh, in_specs=in_specs, out_specs=out_specs, check_vma=False)
```

```python
import functools

import jax
import jax.numpy as jnp
from jax import lax
from jax.experimental import pallas as pl
from jax.experimental.pallas import tpu as pltpu
from jax.sharding import PartitionSpec as P

HEAD = 64
CLUSTER = 128
PAIR = 128
NORM_EPS = 1e-05
EXCLUDED = -1e30
VMEM_BYTES = 24 * 1024 * 1024

F32 = jnp.float32
BF16 = jnp.bfloat16

NN = (((1,), (0,)), ((), ()))
NT = (((1,), (1,)), ((), ()))
TN = (((0,), (0,)), ((), ()))


def dot(a, b, dims=NN):
    return lax.dot_general(a, b, dims, preferred_element_type=F32)


def swap(array, axis, offset, size):
    return lax.ppermute(array, axis, [(i, i ^ offset) for i in range(size)])


def after(array, *earlier):
    return lax.optimization_barrier((array, *earlier))[0]


def block_orders(dp, steps):
    offsets = [0]
    for step in reversed(steps[1:]):
        offsets = offsets + [o ^ step for o in offsets]
    return offsets, [o ^ steps[0] for o in offsets]


def halve_kernel(*refs):
    (keep_ref, got_ref), outs = refs[:2], refs[2:]
    total = keep_ref[...].astype(F32) + got_ref[...].astype(F32)
    if total.shape[0] == 1:
        for out in outs:
            if len(outs) == 1:
                out[...] = total[0]
            elif len(out.shape) == 3:
                out[...] = total[0, : out.shape[0]]
            else:
                out[...] = total[0, -1]
    else:
        half = total.shape[0] // 2
        outs[0][...] = total[:half]
        outs[1][...] = total[half:].astype(BF16)


def halve(keep, got, name):
    shape, half = keep.shape[1:], keep.shape[0] // 2
    if half == 0 and len(shape) == 3:
        parts = [((shape[0] - 1, *shape[1:]), F32, "free"), (shape[1:], F32, "free")]
        return call(halve_kernel, parts, [keep, got], name)
    if half == 0:
        return call(halve_kernel, [(shape, F32, "free")], [keep, got], name)[0]
    return call(halve_kernel, [((half, *shape), F32), ((half, *shape), BF16)], [keep, got], name)


def rows_of(shapes):
    places = []
    for i, (height, width) in enumerate(shapes):
        places += [(i, r, slice(c, c + PAIR)) for r in range(height) for c in range(0, width, PAIR)]
    return places


def pack_kernel(*refs):
    ins, out_ref = refs[:-1], refs[-1]
    out_ref[...] = jnp.zeros(out_ref.shape, F32)
    for k, (i, r, columns) in enumerate(rows_of([ref.shape for ref in ins])):
        out_ref[k : k + 1, :] = ins[i][r : r + 1, columns]


def unpack_kernel(order, shapes, in_ref, *outs):
    for k, (i, r, columns) in enumerate(rows_of(shapes)):
        out, row = order[i][r]
        if outs[out].shape[1] == PAIR:
            row, columns = columns.start // PAIR, slice(0, PAIR)
        outs[out][row : row + 1, columns] = in_ref[k : k + 1, :]


def other_half(array):
    return lax.ppermute(array, "tensor", [(0, 1), (1, 0)])


def call(body, outs, ins, name, scratch=()):
    kinds = [o[2] if len(o) > 2 else "vmem" for o in outs]
    make = {"vmem": pltpu.VMEM, "hbm": pltpu.HBM, "free": jax.ShapeDtypeStruct}
    in_specs, values = [], []
    for x in ins:
        away = isinstance(x, Away)
        in_specs.append(pl.BlockSpec(memory_space=pl.ANY if away else pltpu.VMEM))
        values.append(pltpu.with_memory_space_constraint(x.array, pltpu.HBM) if away else x)
    return pl.pallas_call(
        body,
        out_shape=tuple(make[k](o[0], o[1]) for o, k in zip(outs, kinds)),
        in_specs=in_specs,
        out_specs=tuple(
            pl.BlockSpec(memory_space=pl.ANY if k == "hbm" else pltpu.VMEM) for k in kinds
        ),
        scratch_shapes=list(scratch),
        compiler_params=pltpu.CompilerParams(vmem_limit_bytes=VMEM_BYTES),
        name=name,
    )(*values)


class Away:
    def __init__(self, array):
        self.array = array


def assemble(pieces, whole):
    count = len(pieces)
    me = lax.axis_index("dp") if count > 1 else 0
    for o, piece in enumerate(pieces):
        rows = piece.shape[-2]
        start = pl.multiple_of((me ^ o) * rows, 16) if count > 1 else 0
        if len(piece.shape) == 3:
            whole[:, pl.ds(start, rows), :] = piece[...]
        else:
            whole[pl.ds(start, rows), :] = piece[...]


def norm_rows(v):
    center = jnp.mean(v, axis=-1, keepdims=True)
    offset = v - center
    spread = jnp.mean(offset * offset, axis=-1, keepdims=True)
    scale = lax.rsqrt(spread + NORM_EPS)
    return offset * scale, scale


def norm_back(e, n, scale, gain):
    ea = e * gain
    return scale * (
        ea
        - jnp.mean(ea, axis=-1, keepdims=True)
        - n * jnp.mean(ea * n, axis=-1, keepdims=True)
    )


def admitted_kernel(heads, docs, lengths_ref, perm_ref, bias_ref):
    rows = bias_ref.shape[1]
    spot = lax.broadcasted_iota(jnp.int32, (rows, PAIR), 0)
    lane = lax.broadcasted_iota(jnp.int32, (rows, PAIR), 1)
    doc = jnp.zeros((rows, PAIR), jnp.int32)
    bound = jnp.int32(0)
    for k in range(docs):
        bound = bound + lengths_ref[0, k]
        doc = doc + (spot >= bound).astype(jnp.int32)
    doc_hot = (lane == doc + PAIR // 2).astype(F32)
    cluster_hot = (lane == spot // CLUSTER).astype(BF16)
    place = lax.broadcasted_iota(jnp.int32, (rows, rows), 0)
    for h in range(heads):
        here = (place == perm_ref[h]).astype(BF16)
        key = (dot(here, cluster_hot) + doc_hot).astype(BF16)
        same = dot(key, key, NT)
        bias_ref[h] = jnp.where(same > 1.5, 0.0, EXCLUDED).astype(BF16)


def attention_kernel(count, heads, scale, *refs):
    pieces, refs = refs[:count], refs[count:]
    (tokens_ref, bias_ref, admit_ref, qkv_out, prob_out, attended_ref, out_ref, whole,
     qkv_ref, prob_ref, sems) = refs
    assemble(pieces, whole)
    tokens = tokens_ref[...]
    copies = []

    def away(source, target):
        copies.append(pltpu.make_async_copy(source, target, sems.at[len(copies)]))
        copies[-1].start()

    for s in range(3):
        part = dot(tokens, whole[s])
        if s == 0:
            part = part + bias_ref[0:1, :]
        if s == 2:
            part = part + bias_ref[1:2, :]
        qkv_ref[s] = part.astype(BF16)
        away(qkv_ref.at[s], qkv_out.at[s])
    lane = lax.broadcasted_iota(jnp.int32, (tokens.shape[0], PAIR), 1)
    for pair in range(heads // 2):
        columns = slice(pair * PAIR, (pair + 1) * PAIR)
        q = qkv_ref[0, :, columns]
        k = qkv_ref[1, :, columns]
        v = qkv_ref[2, :, columns]
        mixed = []
        for side in range(2):
            mine = (lane < HEAD) if side == 0 else (lane >= HEAD)
            scores = dot(jnp.where(mine, q, jnp.zeros_like(q)), k, NT) * scale
            scores = scores + admit_ref[2 * pair + side].astype(F32)
            top = jnp.max(scores, axis=-1, keepdims=True)
            terms = jnp.exp(scores - top)
            total = jnp.sum(terms, axis=-1, keepdims=True)
            prob = (terms * (1.0 / total)).astype(BF16)
            prob_ref[2 * pair + side] = prob
            away(prob_ref.at[2 * pair + side], prob_out.at[2 * pair + side])
            mixed.append(dot(prob, v))
        attended_ref[:, columns] = jnp.where(lane < HEAD, mixed[0], mixed[1]).astype(BF16)
    out_ref[...] = dot(attended_ref[...], whole[3], NT).astype(BF16)
    for copy in copies:
        copy.wait()


def feed_kernel(count, *refs):
    pieces, refs = refs[:count], refs[count:]
    (tokens_ref, own_ref, got_ref, out_bias_ref, gain_ref, shift_ref, bias_ref,
     n_ref, scale_ref, low_ref, active_ref, slope_ref, out_ref, whole) = refs
    assemble(pieces, whole)
    attention = own_ref[...].astype(F32) + got_ref[...].astype(F32) + out_bias_ref[0:1, :]
    n, scale = norm_rows(tokens_ref[...].astype(F32) + attention)
    n_ref[...] = n
    scale_ref[...] = jnp.broadcast_to(scale, scale_ref.shape)
    low_ref[...] = (n * gain_ref[0:1, :] + shift_ref[0:1, :]).astype(BF16)
    units = whole.shape[2]
    step = 256
    for start in range(0, units, step):
        part = slice(start, start + step)
        pre = dot(low_ref[...], whole[0, :, part]) + bias_ref[:, part]
        half = 0.5 * (1.0 + lax.erf(pre * (2.0**-0.5)))
        active_ref[:, part] = (pre * half).astype(BF16)
        bell = jnp.exp(-0.5 * pre * pre) * 0.3989422804014327
        slope_ref[:, part] = (half + pre * bell).astype(BF16)
    out_ref[...] = dot(active_ref[...], whole[1], NT).astype(BF16)


def feed_back_kernel(
    whole, n_ref, own_ref, got_ref, out_bias_ref, gain_ref, shift_ref, seed_ref,
    masked_ref, slope_ref, layer_ref, two_ref, low_ref, inner_ref, first_ref, sums_ref, inner_sum_ref,
):
    first = n_ref[...] * gain_ref[0:1, :] + shift_ref[0:1, :]
    feed = own_ref[...].astype(F32) + got_ref[...].astype(F32) + out_bias_ref[1:2, :]
    n, scale = norm_rows(first + feed)
    gain = gain_ref[1:2, :]
    layer_ref[...] = (n * gain + shift_ref[1:2, :]).astype(BF16)
    e = seed_ref[...].astype(F32) * masked_ref[...]
    grad = norm_back(e, n, scale, gain)
    two_ref[...] = grad
    low_ref[...] = grad.astype(BF16)
    sums_ref[0:1, :] = jnp.sum(e * n, axis=0, keepdims=True)
    sums_ref[1:2, :] = jnp.sum(e, axis=0, keepdims=True)
    sums_ref[2:3, :] = jnp.sum(grad, axis=0, keepdims=True)
    units = whole.shape[2]
    step = 256
    for start in range(0, units, step):
        part = slice(start, start + step)
        inner = (dot(low_ref[...], whole[1, :, part]) * slope_ref[:, part].astype(F32)).astype(BF16)
        inner_ref[:, part] = inner
        inner_sum_ref[:, part] = jnp.sum(inner.astype(F32), axis=0, keepdims=True)
    first_ref[...] = dot(inner_ref[...], whole[0], NT).astype(BF16)


def weight_grad_kernel(orders, left_ref, right_ref, keep_ref, send_ref, whole):
    whole[...] = dot(left_ref[...], right_ref[...], TN)
    me = lax.axis_index("dp")
    rows = keep_ref.shape[1]
    for order, target in zip(orders, (keep_ref, send_ref)):
        for k, o in enumerate(order):
            start = pl.multiple_of((me ^ o) * rows, 16)
            target[k] = whole[pl.ds(start, rows), :].astype(BF16)


def norm_one_back_kernel(own_ref, got_ref, two_ref, n_ref, scale_ref, gain_ref, one_ref, low_ref, sums_ref):
    e = own_ref[...].astype(F32) + got_ref[...].astype(F32) + two_ref[...]
    n = n_ref[...]
    grad = norm_back(e, n, scale_ref[:, 0:1], gain_ref[0:1, :])
    one_ref[...] = grad
    low_ref[...] = grad.astype(BF16)
    sums_ref[0:1, :] = jnp.sum(e * n, axis=0, keepdims=True)
    sums_ref[1:2, :] = jnp.sum(e, axis=0, keepdims=True)
    sums_ref[2:3, :] = jnp.sum(grad, axis=0, keepdims=True)


def attention_back_kernel(
    heads, scale, whole_ref, low_ref, qkv_in, prob_in, grads_ref, sums_ref, given, qkv_ref, prob_ref, sems
):
    copies = [pltpu.make_async_copy(qkv_in, qkv_ref, sems.at[heads])]
    for h in range(heads):
        copies.append(pltpu.make_async_copy(prob_in.at[h], prob_ref.at[h], sems.at[h]))
    for copy in copies:
        copy.start()
    given[...] = dot(low_ref[...], whole_ref[3]).astype(BF16)
    lane = lax.broadcasted_iota(jnp.int32, (given.shape[0], PAIR), 1)
    copies[0].wait()
    for pair in range(heads // 2):
        columns = slice(pair * PAIR, (pair + 1) * PAIR)
        q = qkv_ref[0, :, columns]
        k = qkv_ref[1, :, columns]
        v = qkv_ref[2, :, columns]
        d = given[:, columns]
        parts = []
        for side in range(2):
            mine = (lane < HEAD) if side == 0 else (lane >= HEAD)
            copies[1 + 2 * pair + side].wait()
            prob = prob_ref[2 * pair + side]
            d_prob = dot(jnp.where(mine, d, jnp.zeros_like(d)), v, NT)
            wide = prob.astype(F32)
            center = jnp.sum(d_prob * wide, axis=-1, keepdims=True)
            score = (wide * (d_prob - center)).astype(BF16)
            parts.append((dot(score, k), dot(score, q, TN), dot(prob, d, TN)))
        for s in range(3):
            both = jnp.where(lane < HEAD, parts[0][s], parts[1][s])
            if s < 2:
                both = both * scale
            both = both.astype(BF16)
            grads_ref[s, :, columns] = both
            if s != 1:
                sums_ref[s // 2 : s // 2 + 1, columns] = jnp.sum(both.astype(F32), axis=0, keepdims=True)


def input_grad_kernel(whole_ref, grads_ref, out_ref):
    total = dot(grads_ref[0], whole_ref[0], NT)
    total = total + dot(grads_ref[1], whole_ref[1], NT)
    total = total + dot(grads_ref[2], whole_ref[2], NT)
    out_ref[...] = total.astype(BF16)


def mixer_grad_kernel(orders, tokens_ref, grads_ref, low_ref, attended_ref, keep_ref, send_ref, whole):
    me = lax.axis_index("dp")
    rows = keep_ref.shape[2]
    for s in range(4):
        if s < 3:
            whole[...] = dot(tokens_ref[...], grads_ref[s], TN)
        else:
            whole[...] = dot(low_ref[...], attended_ref[...], TN)
        for order, target in zip(orders, (keep_ref, send_ref)):
            for k, o in enumerate(order):
                start = pl.multiple_of((me ^ o) * rows, 16)
                target[k, s] = whole[pl.ds(start, rows), :].astype(BF16)


def add_kernel(own_ref, got_ref, rest_ref, out_ref):
    out_ref[...] = own_ref[...].astype(F32) + got_ref[...].astype(F32) + rest_ref[...]


def plain_grad_kernel(left_ref, right_ref, out_ref):
    out_ref[...] = dot(left_ref[...], right_ref[...], TN)


def shards(
    dp,
    tokens,
    project_weight,
    project_bias,
    output_weight,
    output_bias,
    expand_weight,
    expand_bias,
    shrink_weight,
    norm_gain,
    norm_shift,
    doc_lengths,
    cluster_perm,
    masked,
    out_grad,
):
    rows, width = tokens.shape
    piece_rows, _, columns = project_weight.shape
    units = expand_weight.shape[1]
    heads = columns // HEAD
    scale = HEAD ** (-0.5)
    in_pieces = dp == 16 and piece_rows % 16 == 0

    mixer_shard = jnp.concatenate([project_weight.transpose(1, 0, 2), output_weight.T[None]])
    feed_shard = jnp.stack([expand_weight, shrink_weight.T])
    (admit,) = call(
        functools.partial(admitted_kernel, heads, doc_lengths.shape[1]),
        [((heads, rows, rows), BF16)],
        [doc_lengths, cluster_perm.transpose(1, 0, 2)],
        "admitted",
    )
    if in_pieces:

        def go(array, step, *gate):
            return swap(after(array, *gate) if gate else array, "dp", step, dp)

        def cross(pieces):
            return [go(pieces[o ^ 1], 1) if o & 1 else pieces[o] for o in range(dp)]

        m = {0: mixer_shard}
        m[2] = go(m[0], 2)
        m[8] = go(m[0], 8)
        m[4] = go(m[0], 4)
        m[12] = go(m[8], 4, m[2], admit)
        m[6] = go(m[4], 2)
        m[10] = go(m[8], 2)
        m[14] = go(m[12], 2)
        mixer_all = cross(m)
        f = {0: feed_shard}
        f[8] = go(f[0], 8, m[8])
        f[4] = go(f[0], 4, m[12])
        f[2] = go(f[0], 2, m[14])
        gate = ()
    else:
        gate = ()
        mixer_all = [lax.all_gather(mixer_shard, "dp", axis=1, tiled=True)]
        feed_all = [lax.all_gather(feed_shard, "dp", axis=1, tiled=True)]
    count = len(mixer_all)

    def whole(*shape):
        return pltpu.VMEM(shape, BF16)

    qkv, prob, attended, attention_own, mixer = call(
        functools.partial(attention_kernel, count, heads, scale),
        [
            ((3, rows, columns), BF16, "hbm"),
            ((heads, rows, rows), BF16, "hbm"),
            ((rows, columns), BF16),
            ((rows, width), BF16),
            ((4, width, columns), BF16),
        ],
        [*mixer_all, tokens, after(project_bias, *gate), admit],
        "attention",
        scratch=[
            whole(3, rows, columns), whole(heads, rows, rows), pltpu.SemaphoreType.DMA((3 + heads,)),
        ],
    )
    attention_got = other_half(attention_own)
    if in_pieces:
        f[12] = go(f[8], 4, mixer)
        f[6] = go(f[4], 2, mixer)
        f[10] = go(f[8], 2, mixer)
        f[14] = go(f[12], 2)
        feed_all = cross(f)
    n_one, scale_one, first_low, active_low, slope, feed_own, feed = call(
        functools.partial(feed_kernel, count),
        [
            ((rows, width), F32),
            ((rows, PAIR), F32),
            ((rows, width), BF16),
            ((rows, units), BF16),
            ((rows, units), BF16),
            ((rows, width), BF16),
            ((2, width, units), BF16),
        ],
        [
            *feed_all, tokens, attention_own, attention_got, output_bias,
            norm_gain, norm_shift, expand_bias[None, :],
        ],
        "feed_forward",
    )
    feed_got = other_half(feed_own)
    layer_out, residual_two, feed_low, inner_low, first_own, sums_two, inner_sum = call(
        feed_back_kernel,
        [
            ((rows, width), BF16, "free"),
            ((rows, width), F32),
            ((rows, width), BF16),
            ((rows, units), BF16),
            ((rows, width), BF16),
            ((3, width), F32),
            ((1, units), F32),
        ],
        [
            feed, n_one, feed_own, feed_got, output_bias,
            norm_gain, norm_shift, out_grad, masked.astype(F32)[:, None], slope,
        ],
        "feed_backward",
    )
    first_got = other_half(first_own)

    far = [4, 8]

    def weight_grad(left, right, name, steps=()):
        wide = right.shape[1]
        if in_pieces:
            return call(
                functools.partial(weight_grad_kernel, block_orders(dp, steps)),
                [((dp // 2, piece_rows, wide), BF16)] * 2,
                [left, right],
                name,
                scratch=[pltpu.VMEM((width, wide), F32)],
            )
        (grad,) = call(plain_grad_kernel, [((width, wide), F32, "free")], [left, right], name)
        return lax.psum_scatter(grad, "dp", scatter_dimension=0, tiled=True), grad

    shrink_keep, shrink_send = weight_grad(feed_low, active_low, "shrink_grad", [1, 4, 8, 2])
    expand_keep, expand_send = weight_grad(
        first_low, after(inner_low, shrink_send), "expand_grad", [1, 2, 4, 8]
    )
    gate_one, gate_two = (), ()
    if in_pieces:
        shrink_keep, shrink_send = halve(shrink_keep, swap(shrink_send, "dp", 1, dp), "shrink_sum_core")
        expand_keep, expand_send = halve(expand_keep, swap(expand_send, "dp", 1, dp), "expand_sum_core")
        shrink_got = swap(shrink_send, "dp", 4, dp)
        expand_got = swap(expand_send, "dp", 2, dp)
        gate_one, gate_two = (shrink_send, expand_send), (shrink_got, expand_got)
    residual_one, attention_low, sums_one = call(
        norm_one_back_kernel,
        [((rows, width), F32), ((rows, width), BF16), ((3, width), F32)],
        [first_own, first_got, residual_two, n_one, scale_one, after(norm_gain, *gate_one)],
        "norm_one_backward",
    )
    project_low, project_sums = call(
        functools.partial(attention_back_kernel, heads, scale),
        [((3, rows, columns), BF16), ((2, columns), F32)],
        [mixer, after(attention_low, *gate_two), Away(qkv), Away(prob)],
        "attention_backward",
        scratch=[
            whole(rows, columns), whole(3, rows, columns), whole(heads, rows, rows),
            pltpu.SemaphoreType.DMA((heads + 1,)),
        ],
    )
    vectors = [sums_one, sums_two, inner_sum, project_sums]
    shapes = [v.shape for v in vectors]
    height = -(-sum(v.size for v in vectors) // PAIR // 8) * 8
    (packed,) = call(pack_kernel, [((height, PAIR), F32)], vectors, "pack")

    def input_grad():
        (own,) = call(
            input_grad_kernel, [((rows, width), BF16)], [mixer, project_low], "input_grad"
        )
        return call(
            add_kernel,
            [((rows, width), F32, "free")],
            [own, other_half(own), residual_one],
            "tokens_grad",
        )[0]

    if in_pieces:
        keep, send = call(
            functools.partial(mixer_grad_kernel, block_orders(dp, [1, 2, *far])),
            [((dp // 2, 4, piece_rows, columns), BF16)] * 2,
            [tokens, project_low, attention_low, attended],
            "mixer_grad",
            scratch=[pltpu.VMEM((width, columns), F32)],
        )
        got = swap(send, "dp", 1, dp)
        packed = packed + swap(packed, "dp", 1, dp)
        keep, send = halve(keep, after(got, packed), "mixer_sum_core")
        got = swap(send, "dp", 2, dp)
        packed = packed + swap(packed, "dp", 2, dp)
        tokens_grad = input_grad()
        shrink_keep, shrink_send = halve(shrink_keep, shrink_got, "shrink_sum_4")
        shrink_got = swap(shrink_send, "dp", 8, dp)
        expand_keep, expand_send = halve(expand_keep, expand_got, "expand_sum_2")
        expand_got = swap(expand_send, "dp", 4, dp)
        keep, send = halve(keep, after(got, packed, expand_got), "mixer_sum_2")
        got = swap(send, "dp", 4, dp)
        packed = packed + swap(packed, "dp", 4, dp)
        expand_keep, expand_send = halve(expand_keep, expand_got, "expand_sum_4")
        expand_got = swap(expand_send, "dp", 8, dp)
        shrink_keep, shrink_send = halve(shrink_keep, shrink_got, "shrink_sum_8")
        shrink_got = swap(shrink_send, "dp", 2, dp)
        keep, send = halve(keep, after(got, packed, tokens_grad), "mixer_sum_4")
        got = swap(send, "dp", 8, dp)
        packed = packed + swap(packed, "dp", 8, dp)
        expand_part = halve(expand_keep, expand_got, "expand_sum_8")
        shrink_part = halve(shrink_keep, shrink_got, "shrink_sum_2")
        got = after(got, packed, expand_part, shrink_part)
        project_part, output_part = halve(keep, got, "mixer_sum_8")
    else:
        tokens_grad = input_grad()
        packed = lax.psum(packed, "dp")
        shrink_part, expand_part = shrink_keep, expand_keep
        lefts = [tokens, tokens, tokens, attention_low]
        rights = [project_low[0], project_low[1], project_low[2], attended]
        parts = [weight_grad(l, r, "mixer_grad")[0] for l, r in zip(lefts, rights)]
        project_part, output_part = jnp.stack(parts[:3]), parts[3]
    order = [[(2, 0), (3, 0), (1, 0)], [(2, 1), (3, 1), (1, 1)], [(4, 0)], [(0, 0), (0, 1)]]
    project_total, output_total, gain_total, shift_total, inner_total = call(
        functools.partial(unpack_kernel, order, shapes),
        [
            ((2, columns), F32, "free"),
            ((2, width), F32, "free"),
            ((2, width), F32, "free"),
            ((2, width), F32, "free"),
            ((units // PAIR, PAIR), F32, "free"),
        ],
        [packed],
        "unpack",
    )
    return (
        layer_out,
        tokens_grad,
        project_part.transpose(1, 0, 2),
        project_total,
        output_part.T,
        output_total,
        expand_part,
        inner_total.reshape(units),
        shrink_part.T,
        gain_total,
        shift_total,
    )


def solution(mesh):
    in_specs = (
        P("dp", None),
        P("dp", None, "tensor"),
        P(None, "tensor"),
        P("tensor", "dp"),
        P(),
        P("dp", "tensor"),
        P("tensor"),
        P("tensor", "dp"),
        P(),
        P(),
        P("dp", None),
        P("dp", "tensor", None),
        P("dp"),
        P("dp", None),
    )
    out_specs = (
        P("dp", None),
        P("dp", None),
        P("dp", None, "tensor"),
        P(None, "tensor"),
        P("tensor", "dp"),
        P(),
        P("dp", "tensor"),
        P("tensor"),
        P("tensor", "dp"),
        P(),
        P(),
    )
    body = functools.partial(shards, mesh.shape["dp"])
    return jax.shard_map(body, mesh=mesh, in_specs=in_specs, out_specs=out_specs, check_vma=False)
```

```python
import functools

import jax
import jax.numpy as jnp
from jax import lax
from jax.experimental import pallas as pl
from jax.experimental.pallas import tpu as pltpu
from jax.sharding import PartitionSpec as P

HEAD = 64
CLUSTER = 128
PAIR = 128
NORM_EPS = 1e-05
EXCLUDED = -1e30
VMEM_BYTES = 24 * 1024 * 1024
CUTS = {"y4": 96}

HOPS = {o: (o, o & 12, 2) if o & 2 else (o, 0, o) for o in range(2, 16, 2)}
HOPS.update({o + 1: (o + 1, o, 1) for o in range(0, 16, 2)})
FAR = {"m": 8, "f": 8}
ORDER_BEFORE = (
    "m12", "m6", "m10", "m1", "m3", "m5", "m9", "f8", "f4", "m14", "m7", "f5",
    "m11", "m13", "m15", "f2",
)
ORDER_AFTER = (
    "f12", "f6", "f10", "f1", "f3", "f9", "f14", "f7", "f11", "f13", "f15",
)
SHRINK_STEPS = ((1, 4, 8, 2), (0, 0, 0, 0))
EXPAND_STEPS = ((1, 2, 4, 8), (0, 0, 0, 0))
MIXER_STEPS = ((1, 2, 4, 8), (0, 1, 1, 0))
ORDER_TAIL = (
    "x", "sf", "s", "ef", "e", "xf", "ef", "x", "input", "sf", "s", "e",
    "xf", "x", "s_end", "e_end", "xf", "x",
)
WAITS = {
    "back": ("e2", "s4",),
    "e": ("m15",),
    "e2": ("e",),
    "e8": ("x2b",),
    "f10": ("attention",),
    "f12": ("attention",),
    "f7": ("f12",),
    "f9": ("attention",),
    "m9": ("m8",),
    "x4a": ("x_to_4",),
    "x4b": ("e8",),
    "x_to_2": ("s4", "e2",),
    "y21": ("feed0",),
}

F32 = jnp.float32
BF16 = jnp.bfloat16

NN = (((1,), (0,)), ((), ()))
NT = (((1,), (1,)), ((), ()))
TN = (((0,), (0,)), ((), ()))


def dot(a, b, dims=NN):
    return lax.dot_general(a, b, dims, preferred_element_type=F32)


def swap(array, axis, offset, size):
    return lax.ppermute(array, axis, [(i, i ^ offset) for i in range(size)])


def after(array, *earlier):
    return lax.optimization_barrier((array, *earlier))[0]


class Plan:
    def __init__(self):
        self.made = {}

    def hold(self, name, array):
        gates = [self.made[g] for g in WAITS.get(name, ()) if g in self.made]
        return after(array, *gates) if gates else array

    def note(self, name, array):
        self.made[name] = array
        return array

    def swap(self, name, array, offset):
        return self.note(name, swap(self.hold(name, array), "dp", offset, 16))

    def other(self, name, array, part=None):
        cut = CUTS.get(name, 0)
        if not cut:
            return self.note(name, other_half(self.hold(name, array))) if part != 1 else None
        rows = array[:cut] if part == 0 else array[cut:]
        name = name + "ab"[part]
        return self.note(name, other_half(self.hold(name, rows)))


def offsets_of(steps):
    offsets = [0]
    for step in reversed(steps):
        offsets = offsets + [o ^ step for o in offsets]
    return offsets


def hop(key):
    o, source, step = HOPS[int(key[1:])]
    if o == 12 and FAR[key[0]]:
        source, step = FAR[key[0]], 12 ^ FAR[key[0]]
    return o, source, step


class Reduction:
    def __init__(self, plan, name, kept, sends, steps, split, rider=None):
        self.plan, self.name, self.kept, self.sends = plan, name, kept, sends
        self.steps, self.split, self.rider = list(steps), list(split), rider
        self.arrived = []
        self.count = 8

    def send(self):
        step = self.steps.pop(0)
        count, got = self.count, []
        pieces = len(self.sends)
        for i, array in enumerate(self.sends):
            name = f"{self.name}{step}" + ("ab"[i] if pieces > 1 else "")
            got.append(self.plan.swap(name, array, step))
        if pieces > 1:
            half = count // 2
            self.arrived.append((half, half, got[0], self.rider is not None))
            self.arrived.append((0, half, got[1], False))
        else:
            self.arrived.append((0, count, got[0], self.rider is not None))
        self.step = step
        self.count = count // 2

    def forward(self):
        count = self.count
        split = self.split.pop(0) and count > 1
        ranges = [(count + count // 2, count // 2), (count, count // 2)] if split else [(count, count)]
        needed = [a for a in self.arrived if a[0] + a[1] > count]
        name = f"{self.name}_to_{self.steps[0]}"
        self.sends = self.total(name, ranges, needed)

    def total(self, name, ranges, needed):
        mats = 1 if self.rider is None else 4
        block = self.kept.shape[1:]
        outs = []
        for i, (_, blocks) in enumerate(ranges):
            extra = 1 if self.rider is not None and i == 0 else 0
            outs.append(((blocks * mats + extra, *block), BF16))
        ins = [self.kept, *(a[2] for a in needed)]
        if self.rider is not None:
            outs.append((self.rider.shape, F32))
            ins.append(self.rider)
        ins[1] = self.plan.hold(name, ins[1])
        body = functools.partial(forward_kernel, mats, tuple(ranges), tuple((a[0], a[1], a[3]) for a in needed))
        result = list(call(body, outs, ins, name))
        self.plan.note(name, result[0])
        for i, a in enumerate(self.arrived):
            self.arrived[i] = (a[0], a[1], a[2], False)
        if self.rider is not None:
            self.rider = result.pop()
        return result

    def finish(self, body, outs):
        name = f"{self.name}_end"
        ins = [self.kept, *(a[2] for a in self.arrived)]
        if self.rider is not None:
            ins.append(self.rider)
        ins[1] = self.plan.hold(name, ins[1])
        mats = 1 if self.rider is None else 4
        body = functools.partial(body, mats, tuple((a[0], a[1], a[3]) for a in self.arrived))
        result = call(body, outs, ins, name)
        self.plan.note(name, result[0])
        return result


def ride(vector):
    high = vector.astype(BF16)
    low = (vector - high.astype(F32)).astype(BF16)
    return jnp.concatenate([high, low]), high.astype(F32) + low.astype(F32)


def unride(block):
    half = block.shape[0] // 2
    return block[:half].astype(F32) + block[half:].astype(F32)


def sum_blocks(mats, first, count, kept, gots, places):
    total = kept[first * mats : (first + count) * mats].astype(F32)
    for ref, (start, blocks, _) in zip(gots, places):
        low, high = max(start, first), min(start + blocks, first + count)
        if low < high:
            part = ref[(low - start) * mats : (high - start) * mats].astype(F32)
            pieces = [total[: (low - first) * mats]] if low > first else []
            pieces.append(total[(low - first) * mats : (high - first) * mats] + part)
            if high < first + count:
                pieces.append(total[(high - first) * mats :])
            total = jnp.concatenate(pieces) if len(pieces) > 1 else pieces[0]
    return total


def next_vector(mats, gots, places, rider_ref):
    vector = rider_ref[...]
    for ref, (_, blocks, rides) in zip(gots, places):
        if rides:
            vector = vector + unride(ref[blocks * mats])
    return vector


def forward_kernel(mats, ranges, places, kept, *refs):
    gots, refs = refs[: len(places)], refs[len(places) :]
    if mats > 1:
        rider_ref, outs, rider_out = refs[0], refs[1:-1], refs[-1]
        coded, rider_out[...] = ride(next_vector(mats, gots, places, rider_ref))
        outs[0][ranges[0][1] * mats] = coded
    else:
        outs = refs
    for out, (first, count) in zip(outs, ranges):
        out[: count * mats] = sum_blocks(mats, first, count, kept, gots, places).astype(BF16)


def last_kernel(mats, places, kept, *refs):
    gots, out_ref = refs[:-1], refs[-1]
    out_ref[...] = sum_blocks(mats, 0, 1, kept, gots, places)[0]


def last_mixer_kernel(order, shapes, mats, places, kept, *refs):
    gots, rider_ref, outs = refs[: len(places)], refs[len(places)], refs[len(places) + 1 :]
    total = sum_blocks(mats, 0, 1, kept, gots, places)
    outs[0][...] = total[:-1]
    outs[1][...] = total[-1]
    vector = next_vector(mats, gots, places, rider_ref)
    unpack(order, shapes, vector, outs[2:])


def rows_of(shapes, wide):
    places = []
    for i, (height, width) in enumerate(shapes):
        places += [(i, r, slice(c, c + wide)) for r in range(height) for c in range(0, width, wide)]
    return places


def pack(refs, out_ref):
    wide = out_ref.shape[1]
    out_ref[...] = jnp.zeros(out_ref.shape, F32)
    for k, (i, r, columns) in enumerate(rows_of([ref.shape for ref in refs], wide)):
        out_ref[k : k + 1, :] = refs[i][r : r + 1, columns]


def unpack(order, shapes, vector, outs):
    wide = vector.shape[1]
    for k, (i, r, columns) in enumerate(rows_of(shapes, wide)):
        out, row = order[i][r]
        part = vector[k : k + 1, :]
        if outs[out].shape[1] == PAIR:
            for j in range(wide // PAIR):
                at = columns.start // PAIR + j
                outs[out][at : at + 1, :] = part[:, j * PAIR : (j + 1) * PAIR]
        else:
            outs[out][row : row + 1, columns] = part


def pack_kernel(*refs):
    pack(refs[:-1], refs[-1])


def unpack_kernel(order, shapes, in_ref, *outs):
    unpack(order, shapes, in_ref[...], outs)


def other_half(array):
    return lax.ppermute(array, "tensor", [(0, 1), (1, 0)])


def call(body, outs, ins, name, scratch=()):
    kinds = [o[2] if len(o) > 2 else "vmem" for o in outs]
    make = {"vmem": pltpu.VMEM, "hbm": pltpu.HBM, "free": jax.ShapeDtypeStruct}
    in_specs, values = [], []
    for x in ins:
        away = isinstance(x, Away)
        in_specs.append(pl.BlockSpec(memory_space=pl.ANY if away else pltpu.VMEM))
        values.append(pltpu.with_memory_space_constraint(x.array, pltpu.HBM) if away else x)
    return pl.pallas_call(
        body,
        out_shape=tuple(make[k](o[0], o[1]) for o, k in zip(outs, kinds)),
        in_specs=in_specs,
        out_specs=tuple(
            pl.BlockSpec(memory_space=pl.ANY if k == "hbm" else pltpu.VMEM) for k in kinds
        ),
        scratch_shapes=list(scratch),
        compiler_params=pltpu.CompilerParams(vmem_limit_bytes=VMEM_BYTES),
        name=name,
    )(*values)


class Away:
    def __init__(self, array):
        self.array = array


def assemble(pieces, whole):
    count = len(pieces)
    me = lax.axis_index("dp") if count > 1 else 0
    for o, piece in enumerate(pieces):
        rows = piece.shape[-2]
        start = pl.multiple_of((me ^ o) * rows, 16) if count > 1 else 0
        if len(piece.shape) == 3:
            whole[:, pl.ds(start, rows), :] = piece[...]
        else:
            whole[pl.ds(start, rows), :] = piece[...]


def norm_rows(v):
    center = jnp.mean(v, axis=-1, keepdims=True)
    offset = v - center
    spread = jnp.mean(offset * offset, axis=-1, keepdims=True)
    scale = lax.rsqrt(spread + NORM_EPS)
    return offset * scale, scale


def norm_back(e, n, scale, gain):
    ea = e * gain
    return scale * (
        ea
        - jnp.mean(ea, axis=-1, keepdims=True)
        - n * jnp.mean(ea * n, axis=-1, keepdims=True)
    )


def bundle_kernel(project_ref, output_ref, out_ref, sems):
    one = pltpu.make_async_copy(project_ref, out_ref.at[pl.ds(0, 3)], sems.at[0])
    two = pltpu.make_async_copy(output_ref, out_ref.at[3], sems.at[1])
    one.start()
    two.start()
    one.wait()
    two.wait()


def prepare_kernel(heads, docs, lengths_ref, perm_ref, expand_ref, shrink_ref, bias_ref, feed_ref, sems):
    one = pltpu.make_async_copy(expand_ref, feed_ref.at[0], sems.at[0])
    two = pltpu.make_async_copy(shrink_ref, feed_ref.at[1], sems.at[1])
    one.start()
    two.start()
    rows = bias_ref.shape[1]
    spot = lax.broadcasted_iota(jnp.int32, (rows, PAIR), 0)
    lane = lax.broadcasted_iota(jnp.int32, (rows, PAIR), 1)
    doc = jnp.zeros((rows, PAIR), jnp.int32)
    bound = jnp.int32(0)
    for k in range(docs):
        bound = bound + lengths_ref[0, k]
        doc = doc + (spot >= bound).astype(jnp.int32)
    doc_hot = (lane == doc + PAIR // 2).astype(F32)
    cluster_hot = (lane == spot // CLUSTER).astype(BF16)
    place = lax.broadcasted_iota(jnp.int32, (rows, rows), 0)
    for h in range(heads):
        here = (place == perm_ref[h]).astype(BF16)
        key = (dot(here, cluster_hot) + doc_hot).astype(BF16)
        same = dot(key, key, NT)
        bias_ref[h] = jnp.where(same > 1.5, 0.0, EXCLUDED).astype(BF16)
    one.wait()
    two.wait()


def apart(pair):
    lane = lax.broadcasted_iota(jnp.int32, pair.shape, 1)
    zeros = jnp.zeros_like(pair)
    return jnp.concatenate([jnp.where(lane < HEAD, pair, zeros), jnp.where(lane < HEAD, zeros, pair)])


def attention_kernel(count, heads, scale, *refs):
    pieces, refs = refs[:count], refs[count:]
    (tokens_in, bias_in, admit_ref, qkv_out, prob_out, attended_ref, out_ref, whole,
     qkv_ref, prob_ref, tokens_ref, bias_ref, sems) = refs
    last = sems.shape[0]
    copies = [
        pltpu.make_async_copy(tokens_in, tokens_ref, sems.at[last - 2]),
        pltpu.make_async_copy(bias_in, bias_ref, sems.at[last - 1]),
    ]
    for copy in copies:
        copy.start()
    assemble(pieces, whole)
    for copy in copies:
        copy.wait()
    tokens = tokens_ref[...]
    rows = tokens.shape[0]
    copies = []

    def away(source, target):
        copies.append(pltpu.make_async_copy(source, target, sems.at[len(copies)]))
        copies[-1].start()

    for s in range(3):
        part = dot(tokens, whole[s])
        if s == 0:
            part = part + bias_ref[0:1, :]
        if s == 2:
            part = part + bias_ref[1:2, :]
        qkv_ref[s] = part.astype(BF16)
        away(qkv_ref.at[s], qkv_out.at[s])
    for pair in range(heads // 2):
        columns = slice(pair * PAIR, (pair + 1) * PAIR)
        keys = apart(qkv_ref[1, :, columns])
        scores = dot(keys, qkv_ref[0, :, columns] * scale, NT)
        probs = []
        for side in range(2):
            h = 2 * pair + side
            terms = scores[side * rows : (side + 1) * rows] + admit_ref[h].astype(F32)
            terms = jnp.exp(terms - jnp.max(terms, axis=0, keepdims=True))
            prob = (terms * (1.0 / jnp.sum(terms, axis=0, keepdims=True))).astype(BF16)
            prob_ref[h] = prob
            away(prob_ref.at[h], prob_out.at[h])
            probs.append(prob)
        mixed = dot(apart(qkv_ref[2, :, columns]), jnp.concatenate(probs), TN)
        attended_ref[:, columns] = mixed.T.astype(BF16)
    out_ref[...] = dot(attended_ref[...], whole[3], NT).astype(BF16)
    for copy in copies:
        copy.wait()


def feed_kernel(count, part, gather, *refs):
    if gather:
        pieces, refs = refs[:count], refs[count:]
        whole, refs = refs[-1], refs[:-1]
        assemble(pieces, whole)
    else:
        whole, refs = refs[0], refs[1:]
    (got_ref, tokens_ref, own_ref, out_bias_ref, gain_ref, shift_ref, bias_ref,
     n_ref, scale_ref, low_ref, active_ref, slope_ref, out_ref) = refs
    rows = n_ref.shape[0]
    mine = slice(part * rows, (part + 1) * rows)
    got = got_ref[...] if got_ref.shape[0] == rows else got_ref[mine]
    attention = own_ref[mine].astype(F32) + got.astype(F32) + out_bias_ref[0:1, :]
    n, scale = norm_rows(tokens_ref[mine].astype(F32) + attention)
    n_ref[...] = n
    scale_ref[...] = jnp.broadcast_to(scale, scale_ref.shape)
    low_ref[...] = (n * gain_ref[0:1, :] + shift_ref[0:1, :]).astype(BF16)
    units = whole.shape[2]
    step = 256
    for start in range(0, units, step):
        columns = slice(start, start + step)
        pre = dot(low_ref[...], whole[0, :, columns]) + bias_ref[:, columns]
        half = 0.5 * (1.0 + lax.erf(pre * (2.0**-0.5)))
        active_ref[:, columns] = (pre * half).astype(BF16)
        bell = jnp.exp(-0.5 * pre * pre) * 0.3989422804014327
        slope_ref[:, columns] = (half + pre * bell).astype(BF16)
    out_ref[...] = dot(active_ref[...], whole[1], NT).astype(BF16)


def feed_back_kernel(part, *refs):
    (whole, n_ref, own_ref, got_ref, out_bias_ref, gain_ref, shift_ref, seed_ref, masked_ref, slope_ref,
     *refs) = refs
    if part:
        layer_first, sums_first, inner_first, *refs = refs
    layer_ref, two_ref, low_ref, inner_ref, first_ref, sums_ref, inner_sum_ref = refs
    rows = n_ref.shape[0]
    mine = slice(part * rows, (part + 1) * rows)
    first = n_ref[...] * gain_ref[0:1, :] + shift_ref[0:1, :]
    feed = own_ref[...].astype(F32) + got_ref[...].astype(F32) + out_bias_ref[1:2, :]
    n, scale = norm_rows(first + feed)
    gain = gain_ref[1:2, :]
    layer = (n * gain + shift_ref[1:2, :]).astype(BF16)
    if part:
        layer_ref[:rows] = layer_first[...]
        layer_ref[mine] = layer
    else:
        layer_ref[...] = layer
    e = seed_ref[mine].astype(F32) * masked_ref[mine]
    grad = norm_back(e, n, scale, gain)
    two_ref[...] = grad
    low_ref[...] = grad.astype(BF16)
    for row, values in enumerate((e * n, e, grad)):
        total = jnp.sum(values, axis=0, keepdims=True)
        sums_ref[row : row + 1, :] = total + sums_first[row : row + 1, :] if part else total
    units = whole.shape[2]
    step = 256
    for start in range(0, units, step):
        columns = slice(start, start + step)
        slope = slope_ref[:, columns].astype(F32)
        inner = (dot(low_ref[...], whole[1, :, columns]) * slope).astype(BF16)
        inner_ref[:, columns] = inner
        total = jnp.sum(inner.astype(F32), axis=0, keepdims=True)
        inner_sum_ref[:, columns] = total + inner_first[:, columns] if part else total
    first_ref[...] = dot(inner_ref[...], whole[0], NT).astype(BF16)


def hand_out(offsets, rows, whole, kept_ref, sends, mats=1, mat=0):
    me = lax.axis_index("dp")
    per = 8 // len(sends)
    for k, offset in enumerate(offsets):
        start = pl.multiple_of((me ^ offset) * rows, 16)
        block = whole[pl.ds(start, rows), :]
        if k < 8:
            kept_ref[k * mats + mat] = block
        else:
            part = len(sends) - 1 - (k - 8) // per
            sends[part][(k - 8) % per * mats + mat] = block


def weight_grad_kernel(offsets, left_a, left_b, right_a, right_b, kept_ref, *refs):
    sends, whole = refs[:-1], refs[-1]
    left = jnp.concatenate([left_a[...], left_b[...]])
    right = jnp.concatenate([right_a[...], right_b[...]])
    whole[...] = dot(left, right, TN).astype(BF16)
    hand_out(offsets, kept_ref.shape[1], whole, kept_ref, sends)


def norm_one_back(halves, gain_ref, one_ref, low_ref, sums_ref):
    totals = []
    for part, (own_ref, got_ref, two_ref, n_ref, scale_ref) in enumerate(halves):
        rows = own_ref.shape[0]
        mine = slice(part * rows, (part + 1) * rows)
        e = own_ref[...].astype(F32) + got_ref[...].astype(F32) + two_ref[...]
        n = n_ref[...]
        grad = norm_back(e, n, scale_ref[:, 0:1], gain_ref[0:1, :])
        one_ref[mine] = grad
        low_ref[mine] = grad.astype(BF16)
        totals.append([jnp.sum(values, axis=0, keepdims=True) for values in (e * n, e, grad)])
    for row in range(3):
        sums_ref[row : row + 1, :] = totals[0][row] + totals[1][row]


def attention_back_kernel(heads, scale, *refs):
    halves, refs = (refs[:5], refs[5:10]), refs[10:]
    (gain_ref, whole_ref, qkv_in, prob_in, one_ref, low_ref, norm_sums_ref, grads_ref, sums_ref,
     given, qkv_ref, prob_ref, sems) = refs
    copies = [pltpu.make_async_copy(qkv_in, qkv_ref, sems.at[heads])]
    for h in range(heads):
        copies.append(pltpu.make_async_copy(prob_in.at[h], prob_ref.at[h], sems.at[h]))
    for copy in copies:
        copy.start()
    norm_one_back(halves, gain_ref, one_ref, low_ref, norm_sums_ref)
    given[...] = dot(low_ref[...], whole_ref[3]).astype(BF16)
    rows = given.shape[0]
    lane = lax.broadcasted_iota(jnp.int32, (rows, PAIR), 1)
    copies[0].wait()
    for pair in range(heads // 2):
        columns = slice(pair * PAIR, (pair + 1) * PAIR)
        q = qkv_ref[0, :, columns]
        d = given[:, columns]
        keys = apart(qkv_ref[1, :, columns])
        d_probs = dot(apart(qkv_ref[2, :, columns]), d, NT)
        probs, scores = [], []
        for side in range(2):
            copies[1 + 2 * pair + side].wait()
            prob = prob_ref[2 * pair + side]
            wide = prob.astype(F32)
            d_prob = d_probs[side * rows : (side + 1) * rows]
            center = jnp.sum(d_prob * wide, axis=0, keepdims=True)
            probs.append(prob)
            scores.append((wide * (d_prob - center)).astype(BF16))
        score = jnp.concatenate(scores)
        d_keys = dot(score, q)
        d_values = dot(jnp.concatenate(probs), d)
        d_queries = dot(keys, score, TN).T
        for s, both in enumerate(
            (
                d_queries * scale,
                jnp.where(lane < HEAD, d_keys[:rows], d_keys[rows:]) * scale,
                jnp.where(lane < HEAD, d_values[:rows], d_values[rows:]),
            )
        ):
            both = both.astype(BF16)
            grads_ref[s, :, columns] = both
            if s != 1:
                sums_ref[s // 2 : s // 2 + 1, columns] = jnp.sum(both.astype(F32), axis=0, keepdims=True)


def input_grad_kernel(whole_ref, grads_ref, out_ref):
    total = dot(grads_ref[0], whole_ref[0], NT)
    total = total + dot(grads_ref[1], whole_ref[1], NT)
    total = total + dot(grads_ref[2], whole_ref[2], NT)
    out_ref[...] = total.astype(BF16)


def mixer_grad_kernel(offsets, vectors, tokens_ref, grads_ref, low_ref, attended_ref, *refs):
    vector_refs, (kept_ref, *sends, rider_ref, whole, packed) = refs[:vectors], refs[vectors:]
    pack(vector_refs, packed)
    coded, rider_ref[...] = ride(packed[...])
    sends[0][8 // len(sends) * 4] = coded
    for mat in range(4):
        if mat < 3:
            whole[...] = dot(tokens_ref[...], grads_ref[mat], TN).astype(BF16)
        else:
            whole[...] = dot(low_ref[...], attended_ref[...], TN).astype(BF16)
        hand_out(offsets, kept_ref.shape[1], whole, kept_ref, sends, 4, mat)


def add_kernel(cuts, *refs):
    gots, (own_ref, rest_ref, out_ref) = refs[:cuts], refs[cuts:]
    out_ref[...] = own_ref[...].astype(F32) + joined(gots) + rest_ref[...]


def joined(refs):
    parts = [ref[...].astype(F32) for ref in refs]
    return jnp.concatenate(parts) if len(parts) > 1 else parts[0]


def plain_grad_kernel(left_ref, right_ref, out_ref):
    out_ref[...] = dot(left_ref[...], right_ref[...], TN)


def shards(
    dp,
    tokens,
    project_weight,
    project_bias,
    output_weight,
    output_bias,
    expand_weight,
    expand_bias,
    shrink_weight,
    norm_gain,
    norm_shift,
    doc_lengths,
    cluster_perm,
    masked,
    out_grad,
):
    rows, width = tokens.shape
    piece_rows, _, columns = project_weight.shape
    units = expand_weight.shape[1]
    heads = columns // HEAD
    scale = HEAD**-0.5
    in_pieces = dp == 16 and piece_rows % 16 == 0 and piece_rows == 48 and columns == 384
    plan = Plan()
    note, hold = plan.note, plan.hold

    def whole(*shape):
        return pltpu.VMEM(shape, BF16)

    def sems(count):
        return pltpu.SemaphoreType.DMA((count,))

    (mixer_shard,) = call(
        bundle_kernel,
        [((4, piece_rows, columns), BF16)],
        [Away(project_weight.transpose(1, 0, 2)), Away(output_weight.T)],
        "bundle",
        scratch=[sems(2)],
    )
    m = {0: mixer_shard}
    if in_pieces:
        for o, source, step in ((8, 0, 8), (2, 0, 2), (4, 0, 4)):
            m[o] = plan.swap(f"m{o}", m[source], step)
    admit, feed_shard = call(
        functools.partial(prepare_kernel, heads, doc_lengths.shape[1]),
        [((heads, rows, rows), BF16), ((2, piece_rows, units), BF16)],
        [hold("prepare", doc_lengths), cluster_perm.transpose(1, 0, 2), Away(expand_weight), Away(shrink_weight.T)],
        "prepare",
        scratch=[sems(2)],
    )
    note("prepare", admit)
    f = {0: feed_shard}
    if in_pieces:
        for key in ORDER_BEFORE:
            pieces = m if key[0] == "m" else f
            o, source, step = hop(key)
            pieces[o] = plan.swap(key, pieces[source], step)
        mixer_all = [m[o] for o in range(dp)]
    else:
        mixer_all = [lax.all_gather(mixer_shard, "dp", axis=1, tiled=True)]
        feed_all = [lax.all_gather(feed_shard, "dp", axis=1, tiled=True)]
    count = len(mixer_all)

    qkv, prob, attended, attention_own, mixer = call(
        functools.partial(attention_kernel, count, heads, scale),
        [
            ((3, rows, columns), BF16, "hbm"),
            ((heads, rows, rows), BF16, "hbm"),
            ((rows, columns), BF16),
            ((rows, width), BF16),
            ((4, width, columns), BF16),
        ],
        [*mixer_all, Away(tokens), Away(project_bias), hold("attention", admit)],
        "attention",
        scratch=[
            whole(3, rows, columns), whole(heads, rows, rows), whole(rows, width),
            pltpu.VMEM((2, columns), F32), sems(5 + heads),
        ],
    )
    note("attention", mixer)
    attention_got = [plan.other("y1", attention_own, 0)]
    attention_got.append(plan.other("y1", attention_own, 1))
    attention_got = [x for x in attention_got if x is not None]
    if in_pieces:
        for key in ORDER_AFTER:
            o, source, step = hop(key)
            f[o] = plan.swap(key, f[source], step)
        feed_all = [f[o] for o in range(dp)]
    half_rows = rows // 2
    forward, feed = [], None
    for part in range(2):
        got = attention_got[part] if len(attention_got) == 2 else attention_got[0]
        outs = [
            ((half_rows, width), F32),
            ((half_rows, PAIR), F32),
            ((half_rows, width), BF16),
            ((half_rows, units), BF16),
            ((half_rows, units), BF16),
            ((half_rows, width), BF16),
        ]
        bias = hold(f"feed{part}", output_bias)
        weights = [feed] if part else feed_all
        result = call(
            functools.partial(feed_kernel, count, part, not part),
            outs if part else [*outs, ((2, width, units), BF16)],
            [*weights, got, tokens, attention_own, bias, norm_gain, norm_shift, expand_bias[None, :]],
            f"feed_forward_{part}",
        )
        if not part:
            *result, feed = result
        note(f"feed{part}", result[5])
        forward.append((*result, plan.other(f"y2{part}", result[5])))
    back, seed = [], masked.astype(F32)[:, None]
    for part in range(2):
        n_one, scale_one, first_low, active_low, slope, feed_own, feed_got = forward[part]
        result = call(
            functools.partial(feed_back_kernel, part),
            [
                ((rows, width), BF16, "free") if part else ((half_rows, width), BF16),
                ((half_rows, width), F32),
                ((half_rows, width), BF16),
                ((half_rows, units), BF16),
                ((half_rows, width), BF16),
                ((3, width), F32),
                ((1, units), F32),
            ],
            [
                feed, n_one, feed_own, feed_got, hold(f"feed_back{part}", output_bias), norm_gain, norm_shift,
                out_grad, seed, slope, *((back[0][0], *back[0][5:7]) if part else ()),
            ],
            f"feed_backward_{part}",
        )
        note(f"feed_back{part}", result[4])
        back.append((*result, plan.other(f"y3{part}", result[4])))
    layer_out, sums_two, inner_sum = back[1][0], back[1][5], back[1][6]

    def plain_grad(left, right, name):
        (grad,) = call(plain_grad_kernel, [((width, right.shape[1]), F32, "free")], [left, right], name)
        return lax.psum_scatter(grad, "dp", scatter_dimension=0, tiled=True)

    grads_of = (
        ([x[2] for x in back], [x[3] for x in forward]),
        ([x[2] for x in forward], [x[3] for x in back]),
    )

    def weight_grad(left, right, name, steps, split):
        wide = right[0].shape[1]
        parts = 2 if split[0] else 1
        outs = [((8, piece_rows, wide), BF16)] + [((8 // parts, piece_rows, wide), BF16)] * parts
        kept, *sends = call(
            functools.partial(weight_grad_kernel, offsets_of(steps)),
            outs,
            [*left, right[0], hold(name, right[1])],
            name,
            scratch=[whole(width, wide)],
        )
        note(name, kept)
        return Reduction(plan, name, kept, sends, steps, split[1:])

    if in_pieces:
        shrink = weight_grad(*grads_of[0], "s", *SHRINK_STEPS)
        expand = weight_grad(*grads_of[1], "e", *EXPAND_STEPS)
        shrink.send()
        expand.send()
        shrink.forward()
        shrink.send()
        expand.forward()
        expand.send()
    residual_one, attention_low, sums_one, project_low, project_sums = call(
        functools.partial(attention_back_kernel, heads, scale),
        [
            ((rows, width), F32),
            ((rows, width), BF16),
            ((3, width), F32),
            ((3, rows, columns), BF16),
            ((2, columns), F32),
        ],
        [
            *(x for p in range(2) for x in (back[p][4], back[p][7], back[p][1], *forward[p][:2])),
            hold("back", norm_gain), mixer, Away(qkv), Away(prob),
        ],
        "attention_backward",
        scratch=[
            whole(rows, columns), whole(3, rows, columns), whole(heads, rows, rows), sems(heads + 1),
        ],
    )
    note("back", project_low)
    vectors = [sums_one, sums_two, inner_sum, project_sums]
    shapes = [v.shape for v in vectors]
    order = [[(2, 0), (3, 0), (1, 0)], [(2, 1), (3, 1), (1, 1)], [(4, 0)], [(0, 0), (0, 1)]]
    vector_outs = [
        ((2, columns), F32, "free"),
        ((2, width), F32, "free"),
        ((2, width), F32, "free"),
        ((2, width), F32, "free"),
        ((units // PAIR, PAIR), F32, "free"),
    ]

    def input_grad():
        (own,) = call(
            input_grad_kernel,
            [((rows, width), BF16)],
            [mixer, hold("input", project_low)],
            "input_grad",
        )
        note("input", own)
        gots = [plan.other("y4", own, 0)]
        gots.append(plan.other("y4", own, 1))
        gots = [x for x in gots if x is not None]
        (result,) = call(
            functools.partial(add_kernel, len(gots)),
            [((rows, width), F32, "free")],
            [*gots, own, hold("tokens", residual_one)],
            "tokens_grad",
        )
        return note("tokens", result)

    if in_pieces:
        steps, split = MIXER_STEPS
        parts = 2 if split[0] else 1
        half = piece_rows // 2
        kept, *sends, rider = call(
            functools.partial(mixer_grad_kernel, offsets_of(steps), len(vectors)),
            [((32, piece_rows, columns), BF16)]
            + [((8 // parts * 4 + (i == 0), piece_rows, columns), BF16) for i in range(parts)]
            + [((half, columns), F32)],
            [tokens, hold("x", project_low), attention_low, attended, *vectors],
            "mixer_grad",
            scratch=[whole(width, columns), pltpu.VMEM((half, columns), F32)],
        )
        note("x", kept)
        mixed = Reduction(plan, "x", kept, sends, steps, split[1:], rider)
        parts_of = {"s": shrink, "e": expand, "x": mixed}
        block = (piece_rows, units)
        for key in ORDER_TAIL:
            if key == "input":
                tokens_grad = input_grad()
            elif key == "s_end":
                (shrink_part,) = shrink.finish(last_kernel, [(block, F32, "free")])
            elif key == "e_end":
                (expand_part,) = expand.finish(last_kernel, [(block, F32, "free")])
            elif key[1:] == "f":
                parts_of[key[0]].forward()
            else:
                parts_of[key[0]].send()
        project_part, output_part, *totals = mixed.finish(
            functools.partial(last_mixer_kernel, order, shapes),
            [((3, piece_rows, columns), F32, "free"), ((piece_rows, columns), F32, "free"), *vector_outs],
        )
    else:
        tokens_grad = input_grad()
        height = -(-sum(v.size for v in vectors) // PAIR // 8) * 8
        (packed,) = call(pack_kernel, [((height, PAIR), F32)], vectors, "pack")
        totals = call(
            functools.partial(unpack_kernel, order, shapes), vector_outs, [lax.psum(packed, "dp")], "unpack"
        )
        shrink_part, expand_part = (
            plain_grad(jnp.concatenate(left), jnp.concatenate(right), name)
            for (left, right), name in zip(grads_of, ("shrink_grad", "expand_grad"))
        )
        project_part = jnp.stack([plain_grad(tokens, project_low[s], "project_grad") for s in range(3)])
        output_part = plain_grad(attention_low, attended, "output_grad")
    project_total, output_total, gain_total, shift_total, inner_total = totals
    return (
        layer_out,
        tokens_grad,
        project_part.transpose(1, 0, 2),
        project_total,
        output_part.T,
        output_total,
        expand_part,
        inner_total.reshape(units),
        shrink_part.T,
        gain_total,
        shift_total,
    )


def solution(mesh):
    in_specs = (
        P("dp", None),
        P("dp", None, "tensor"),
        P(None, "tensor"),
        P("tensor", "dp"),
        P(),
        P("dp", "tensor"),
        P("tensor"),
        P("tensor", "dp"),
        P(),
        P(),
        P("dp", None),
        P("dp", "tensor", None),
        P("dp"),
        P("dp", None),
    )
    out_specs = (
        P("dp", None),
        P("dp", None),
        P("dp", None, "tensor"),
        P(None, "tensor"),
        P("tensor", "dp"),
        P(),
        P("dp", "tensor"),
        P("tensor"),
        P("tensor", "dp"),
        P(),
        P(),
    )
    body = functools.partial(shards, mesh.shape["dp"])
    return jax.shard_map(body, mesh=mesh, in_specs=in_specs, out_specs=out_specs, check_vma=False)
```

```python
import functools

import jax
import jax.numpy as jnp
from jax import lax
from jax.experimental import pallas as pl
from jax.experimental.pallas import tpu as pltpu
from jax.sharding import PartitionSpec as P

HEAD = 64
CLUSTER = 128
PAIR = 128
NORM_EPS = 1e-05
EXCLUDED = -1e30
VMEM_BYTES = 24 * 1024 * 1024
CUTS = {"y1": 192, "y4": 96}

HOPS = {o: (o, o & 12, 2) if o & 2 else (o, 0, o) for o in range(2, 16, 2)}
HOPS.update({o + 1: (o + 1, o, 1) for o in range(0, 16, 2)})
FAR = {"m": 8, "f": 8}
ORDER_BEFORE = (
    "m12", "m6", "m10", "m1", "m3", "m5", "m9", "f8", "f4", "m14", "m7", "f5",
    "m11", "m13", "m15", "f2",
)
ORDER_AFTER = (
    "f12", "f6", "f10", "f1", "f3", "f9", "f14", "f7", "f11", "f13", "f15",
)
SHRINK_STEPS = ((1, 4, 8, 2), (1, 1, 1, 1))
EXPAND_STEPS = ((1, 2, 4, 8), (1, 1, 1, 1))
MIXER_STEPS = ((1, 2, 4, 8), (4, 2, 2, 1))
ORDER_TAIL = (
    "x", "sf", "s", "ef", "e", "xf", "ef", "x", "input", "e", "sf", "s",
    "xf", "x", "s_end", "e_end", "xf", "x",
)
WAITS = {
    "e": ("m15",),
    "e1": ("y30",),
    "e2": ("f7",),
    "e4": ("feed_back0",),
    "e8": ("x2b", "y4a",),
    "e_end": ("x4a",),
    "e_to_2": ("s_to_4",),
    "f10": ("attention",),
    "f12": ("attention",),
    "f7": ("f4",),
    "f9": ("attention",),
    "m9": ("m8",),
    "tokens": ("x_to_2",),
    "x4a": ("x_to_4",),
    "x_to_2": ("s4", "e2",),
    "x_to_4": ("e4", "x1c",),
    "x_to_8": ("x2b",),
    "y21": ("feed0",),
    "y4b": ("input",),
}

F32 = jnp.float32
BF16 = jnp.bfloat16

NN = (((1,), (0,)), ((), ()))
NT = (((1,), (1,)), ((), ()))
TN = (((0,), (0,)), ((), ()))


def dot(a, b, dims=NN):
    return lax.dot_general(a, b, dims, preferred_element_type=F32)


def swap(array, axis, offset, size):
    return lax.ppermute(array, axis, [(i, i ^ offset) for i in range(size)])


def after(array, *earlier):
    return lax.optimization_barrier((array, *earlier))[0]


class Plan:
    def __init__(self):
        self.made = {}

    def hold(self, name, array):
        gates = [self.made[g] for g in WAITS.get(name, ()) if g in self.made]
        return after(array, *gates) if gates else array

    def note(self, name, array):
        self.made[name] = array
        return array

    def swap(self, name, array, offset):
        return self.note(name, swap(self.hold(name, array), "dp", offset, 16))

    def other(self, name, array, part=None):
        cut = CUTS.get(name, 0)
        if not cut:
            return self.note(name, other_half(self.hold(name, array))) if part != 1 else None
        rows = array[:cut] if part == 0 else array[cut:]
        name = name + "ab"[part]
        return self.note(name, other_half(self.hold(name, rows)))


def offsets_of(steps):
    offsets = [0]
    for step in reversed(steps):
        offsets = offsets + [o ^ step for o in offsets]
    return offsets


def hop(key):
    o, source, step = HOPS[int(key[1:])]
    if o == 12 and FAR[key[0]]:
        source, step = FAR[key[0]], 12 ^ FAR[key[0]]
    return o, source, step


class Reduction:
    def __init__(self, plan, name, kept, sends, steps, split, rider=None):
        self.plan, self.name, self.kept, self.sends = plan, name, kept, sends
        self.steps, self.split, self.rider = list(steps), list(split), rider
        self.arrived = []
        self.count = 8

    def send(self):
        step = self.steps.pop(0)
        count = self.count
        pieces = len(self.sends)
        per = count // pieces
        for i, array in enumerate(self.sends):
            name = f"{self.name}{step}" + ("abcd"[i] if pieces > 1 else "")
            got = self.plan.swap(name, array, step)
            self.arrived.append((count - (i + 1) * per, per, got, self.rider is not None and i == 0))
        self.step = step
        self.count = count // 2

    def forward(self):
        count = self.count
        parts = min(self.split.pop(0), count)
        per = count // parts
        ranges = [(2 * count - (i + 1) * per, per) for i in range(parts)]
        needed = [a for a in self.arrived if a[0] + a[1] > count]
        name = f"{self.name}_to_{self.steps[0]}"
        self.sends = self.total(name, ranges, needed)

    def total(self, name, ranges, needed):
        mats = 1 if self.rider is None else 4
        block = self.kept.shape[1:]
        outs = []
        for i, (_, blocks) in enumerate(ranges):
            extra = 1 if self.rider is not None and i == 0 else 0
            outs.append(((blocks * mats + extra, *block), BF16))
        ins = [self.kept, *(a[2] for a in needed)]
        if self.rider is not None:
            outs.append((self.rider.shape, F32))
            ins.append(self.rider)
        ins[1] = self.plan.hold(name, ins[1])
        body = functools.partial(forward_kernel, mats, tuple(ranges), tuple((a[0], a[1], a[3]) for a in needed))
        result = list(call(body, outs, ins, name))
        self.plan.note(name, result[0])
        for i, a in enumerate(self.arrived):
            self.arrived[i] = (a[0], a[1], a[2], False)
        if self.rider is not None:
            self.rider = result.pop()
        return result

    def finish(self, body, outs):
        name = f"{self.name}_end"
        ins = [self.kept, *(a[2] for a in self.arrived)]
        if self.rider is not None:
            ins.append(self.rider)
        ins[1] = self.plan.hold(name, ins[1])
        mats = 1 if self.rider is None else 4
        body = functools.partial(body, mats, tuple((a[0], a[1], a[3]) for a in self.arrived))
        result = call(body, outs, ins, name)
        self.plan.note(name, result[0])
        return result


def ride(vector):
    high = vector.astype(BF16)
    low = (vector - high.astype(F32)).astype(BF16)
    return jnp.concatenate([high, low]), high.astype(F32) + low.astype(F32)


def unride(block):
    half = block.shape[0] // 2
    return block[:half].astype(F32) + block[half:].astype(F32)


def sum_blocks(mats, first, count, kept, gots, places):
    total = kept[first * mats : (first + count) * mats].astype(F32)
    for ref, (start, blocks, _) in zip(gots, places):
        low, high = max(start, first), min(start + blocks, first + count)
        if low < high:
            part = ref[(low - start) * mats : (high - start) * mats].astype(F32)
            pieces = [total[: (low - first) * mats]] if low > first else []
            pieces.append(total[(low - first) * mats : (high - first) * mats] + part)
            if high < first + count:
                pieces.append(total[(high - first) * mats :])
            total = jnp.concatenate(pieces) if len(pieces) > 1 else pieces[0]
    return total


def next_vector(mats, gots, places, rider_ref):
    vector = rider_ref[...]
    for ref, (_, blocks, rides) in zip(gots, places):
        if rides:
            vector = vector + unride(ref[blocks * mats])
    return vector


def forward_kernel(mats, ranges, places, kept, *refs):
    gots, refs = refs[: len(places)], refs[len(places) :]
    if mats > 1:
        rider_ref, outs, rider_out = refs[0], refs[1:-1], refs[-1]
        coded, rider_out[...] = ride(next_vector(mats, gots, places, rider_ref))
        outs[0][ranges[0][1] * mats] = coded
    else:
        outs = refs
    for out, (first, count) in zip(outs, ranges):
        out[: count * mats] = sum_blocks(mats, first, count, kept, gots, places).astype(BF16)


def last_kernel(mats, places, kept, *refs):
    gots, out_ref = refs[:-1], refs[-1]
    out_ref[...] = sum_blocks(mats, 0, 1, kept, gots, places)[0]


def last_mixer_kernel(order, shapes, mats, places, kept, *refs):
    gots, rider_ref, outs = refs[: len(places)], refs[len(places)], refs[len(places) + 1 :]
    total = sum_blocks(mats, 0, 1, kept, gots, places)
    outs[0][...] = total[:-1]
    outs[1][...] = total[-1]
    vector = next_vector(mats, gots, places, rider_ref)
    unpack(order, shapes, vector, outs[2:])


def rows_of(shapes, wide):
    places = []
    for i, (height, width) in enumerate(shapes):
        places += [(i, r, slice(c, c + wide)) for r in range(height) for c in range(0, width, wide)]
    return places


def pack(refs, out_ref):
    wide = out_ref.shape[1]
    out_ref[...] = jnp.zeros(out_ref.shape, F32)
    for k, (i, r, columns) in enumerate(rows_of([ref.shape for ref in refs], wide)):
        out_ref[k : k + 1, :] = refs[i][r : r + 1, columns]


def unpack(order, shapes, vector, outs):
    wide = vector.shape[1]
    for k, (i, r, columns) in enumerate(rows_of(shapes, wide)):
        out, row = order[i][r]
        part = vector[k : k + 1, :]
        if outs[out].shape[1] == PAIR:
            for j in range(wide // PAIR):
                at = columns.start // PAIR + j
                outs[out][at : at + 1, :] = part[:, j * PAIR : (j + 1) * PAIR]
        else:
            outs[out][row : row + 1, columns] = part


def pack_kernel(*refs):
    pack(refs[:-1], refs[-1])


def unpack_kernel(order, shapes, in_ref, *outs):
    unpack(order, shapes, in_ref[...], outs)


def other_half(array):
    return lax.ppermute(array, "tensor", [(0, 1), (1, 0)])


def call(body, outs, ins, name, scratch=()):
    kinds = [o[2] if len(o) > 2 else "vmem" for o in outs]
    make = {"vmem": pltpu.VMEM, "hbm": pltpu.HBM, "free": jax.ShapeDtypeStruct}
    in_specs, values = [], []
    for x in ins:
        away = isinstance(x, Away)
        in_specs.append(pl.BlockSpec(memory_space=pl.ANY if away else pltpu.VMEM))
        values.append(pltpu.with_memory_space_constraint(x.array, pltpu.HBM) if away else x)
    return pl.pallas_call(
        body,
        out_shape=tuple(make[k](o[0], o[1]) for o, k in zip(outs, kinds)),
        in_specs=in_specs,
        out_specs=tuple(
            pl.BlockSpec(memory_space=pl.ANY if k == "hbm" else pltpu.VMEM) for k in kinds
        ),
        scratch_shapes=list(scratch),
        compiler_params=pltpu.CompilerParams(vmem_limit_bytes=VMEM_BYTES),
        name=name,
    )(*values)


class Away:
    def __init__(self, array):
        self.array = array


def assemble(pieces, whole):
    count = len(pieces)
    me = lax.axis_index("dp") if count > 1 else 0
    for o, piece in enumerate(pieces):
        rows = piece.shape[-2]
        start = pl.multiple_of((me ^ o) * rows, 16) if count > 1 else 0
        if len(piece.shape) == 3:
            whole[:, pl.ds(start, rows), :] = piece[...]
        else:
            whole[pl.ds(start, rows), :] = piece[...]


def norm_rows(v):
    center = jnp.mean(v, axis=-1, keepdims=True)
    offset = v - center
    spread = jnp.mean(offset * offset, axis=-1, keepdims=True)
    scale = lax.rsqrt(spread + NORM_EPS)
    return offset * scale, scale


def norm_back(e, n, scale, gain):
    ea = e * gain
    return scale * (
        ea
        - jnp.mean(ea, axis=-1, keepdims=True)
        - n * jnp.mean(ea * n, axis=-1, keepdims=True)
    )


def bundle_kernel(project_ref, output_ref, out_ref, sems):
    one = pltpu.make_async_copy(project_ref, out_ref.at[pl.ds(0, 3)], sems.at[0])
    two = pltpu.make_async_copy(output_ref, out_ref.at[3], sems.at[1])
    one.start()
    two.start()
    one.wait()
    two.wait()


def prepare_kernel(heads, docs, lengths_ref, perm_ref, expand_ref, shrink_ref, bias_ref, feed_ref, sems):
    one = pltpu.make_async_copy(expand_ref, feed_ref.at[0], sems.at[0])
    two = pltpu.make_async_copy(shrink_ref, feed_ref.at[1], sems.at[1])
    one.start()
    two.start()
    rows = bias_ref.shape[1]
    spot = lax.broadcasted_iota(jnp.int32, (rows, PAIR), 0)
    lane = lax.broadcasted_iota(jnp.int32, (rows, PAIR), 1)
    doc = jnp.zeros((rows, PAIR), jnp.int32)
    bound = jnp.int32(0)
    for k in range(docs):
        bound = bound + lengths_ref[0, k]
        doc = doc + (spot >= bound).astype(jnp.int32)
    doc_hot = (lane == doc + PAIR // 2).astype(F32)
    cluster_hot = (lane == spot // CLUSTER).astype(BF16)
    place = lax.broadcasted_iota(jnp.int32, (rows, rows), 0)
    for h in range(heads):
        here = (place == perm_ref[h]).astype(BF16)
        key = (dot(here, cluster_hot) + doc_hot).astype(BF16)
        same = dot(key, key, NT)
        bias_ref[h] = jnp.where(same > 1.5, 0.0, EXCLUDED).astype(BF16)
    one.wait()
    two.wait()


def apart(pair):
    lane = lax.broadcasted_iota(jnp.int32, pair.shape, 1)
    zeros = jnp.zeros_like(pair)
    return jnp.concatenate([jnp.where(lane < HEAD, pair, zeros), jnp.where(lane < HEAD, zeros, pair)])


def attention_kernel(count, heads, scale, *refs):
    pieces, refs = refs[:count], refs[count:]
    (tokens_in, bias_in, admit_ref, qkv_out, prob_out, attended_ref, out_ref, whole,
     qkv_ref, prob_ref, tokens_ref, bias_ref, sems) = refs
    last = sems.shape[0]
    copies = [
        pltpu.make_async_copy(tokens_in, tokens_ref, sems.at[last - 2]),
        pltpu.make_async_copy(bias_in, bias_ref, sems.at[last - 1]),
    ]
    for copy in copies:
        copy.start()
    assemble(pieces, whole)
    for copy in copies:
        copy.wait()
    tokens = tokens_ref[...]
    rows = tokens.shape[0]
    copies = []

    def away(source, target):
        copies.append(pltpu.make_async_copy(source, target, sems.at[len(copies)]))
        copies[-1].start()

    for s in range(3):
        part = dot(tokens, whole[s])
        if s == 0:
            part = part + bias_ref[0:1, :]
        if s == 2:
            part = part + bias_ref[1:2, :]
        qkv_ref[s] = part.astype(BF16)
        away(qkv_ref.at[s], qkv_out.at[s])
    for pair in range(heads // 2):
        columns = slice(pair * PAIR, (pair + 1) * PAIR)
        keys = apart(qkv_ref[1, :, columns])
        scores = dot(keys, qkv_ref[0, :, columns] * scale, NT)
        probs = []
        for side in range(2):
            h = 2 * pair + side
            terms = scores[side * rows : (side + 1) * rows] + admit_ref[h].astype(F32)
            terms = jnp.exp(terms - jnp.max(terms, axis=0, keepdims=True))
            prob = (terms * (1.0 / jnp.sum(terms, axis=0, keepdims=True))).astype(BF16)
            prob_ref[h] = prob
            away(prob_ref.at[h], prob_out.at[h])
            probs.append(prob)
        mixed = dot(apart(qkv_ref[2, :, columns]), jnp.concatenate(probs), TN)
        attended_ref[:, columns] = mixed.T.astype(BF16)
    out_ref[...] = dot(attended_ref[...], whole[3], NT).astype(BF16)
    for copy in copies:
        copy.wait()


def feed_kernel(count, part, gather, *refs):
    if gather:
        pieces, refs = refs[:count], refs[count:]
        whole, refs = refs[-1], refs[:-1]
        assemble(pieces, whole)
    else:
        whole, refs = refs[0], refs[1:]
    (got_ref, tokens_ref, own_ref, out_bias_ref, gain_ref, shift_ref, bias_ref,
     n_ref, scale_ref, low_ref, active_ref, slope_ref, out_ref) = refs
    rows = n_ref.shape[0]
    mine = slice(part * rows, (part + 1) * rows)
    got = got_ref[...] if got_ref.shape[0] == rows else got_ref[mine]
    attention = own_ref[mine].astype(F32) + got.astype(F32) + out_bias_ref[0:1, :]
    n, scale = norm_rows(tokens_ref[mine].astype(F32) + attention)
    n_ref[...] = n
    scale_ref[...] = jnp.broadcast_to(scale, scale_ref.shape)
    low_ref[...] = (n * gain_ref[0:1, :] + shift_ref[0:1, :]).astype(BF16)
    units = whole.shape[2]
    step = 256
    for start in range(0, units, step):
        columns = slice(start, start + step)
        pre = dot(low_ref[...], whole[0, :, columns]) + bias_ref[:, columns]
        half = 0.5 * (1.0 + lax.erf(pre * (2.0**-0.5)))
        active_ref[:, columns] = (pre * half).astype(BF16)
        bell = jnp.exp(-0.5 * pre * pre) * 0.3989422804014327
        slope_ref[:, columns] = (half + pre * bell).astype(BF16)
    out_ref[...] = dot(active_ref[...], whole[1], NT).astype(BF16)


def feed_back_kernel(part, *refs):
    (whole, n_ref, own_ref, got_ref, out_bias_ref, gain_ref, shift_ref, seed_ref, masked_ref, slope_ref,
     *refs) = refs
    if part:
        layer_first, sums_first, inner_first, *refs = refs
    layer_ref, two_ref, low_ref, inner_ref, first_ref, sums_ref, inner_sum_ref = refs
    rows = n_ref.shape[0]
    mine = slice(part * rows, (part + 1) * rows)
    first = n_ref[...] * gain_ref[0:1, :] + shift_ref[0:1, :]
    feed = own_ref[...].astype(F32) + got_ref[...].astype(F32) + out_bias_ref[1:2, :]
    n, scale = norm_rows(first + feed)
    gain = gain_ref[1:2, :]
    layer = (n * gain + shift_ref[1:2, :]).astype(BF16)
    if part:
        layer_ref[:rows] = layer_first[...]
        layer_ref[mine] = layer
    else:
        layer_ref[...] = layer
    e = seed_ref[mine].astype(F32) * masked_ref[mine]
    grad = norm_back(e, n, scale, gain)
    two_ref[...] = grad
    low_ref[...] = grad.astype(BF16)
    for row, values in enumerate((e * n, e, grad)):
        total = jnp.sum(values, axis=0, keepdims=True)
        sums_ref[row : row + 1, :] = total + sums_first[row : row + 1, :] if part else total
    units = whole.shape[2]
    step = 256
    for start in range(0, units, step):
        columns = slice(start, start + step)
        slope = slope_ref[:, columns].astype(F32)
        inner = (dot(low_ref[...], whole[1, :, columns]) * slope).astype(BF16)
        inner_ref[:, columns] = inner
        total = jnp.sum(inner.astype(F32), axis=0, keepdims=True)
        inner_sum_ref[:, columns] = total + inner_first[:, columns] if part else total
    first_ref[...] = dot(inner_ref[...], whole[0], NT).astype(BF16)


def hand_out(offsets, rows, whole, kept_ref, sends, mats=1, mat=0):
    me = lax.axis_index("dp")
    per = 8 // len(sends)
    for k, offset in enumerate(offsets):
        start = pl.multiple_of((me ^ offset) * rows, 16)
        block = whole[pl.ds(start, rows), :]
        if k < 8:
            kept_ref[k * mats + mat] = block
        else:
            part = len(sends) - 1 - (k - 8) // per
            sends[part][(k - 8) % per * mats + mat] = block


def weight_grad_kernel(offsets, left_a, left_b, right_a, right_b, kept_ref, *refs):
    sends, whole = refs[:-1], refs[-1]
    left = jnp.concatenate([left_a[...], left_b[...]])
    right = jnp.concatenate([right_a[...], right_b[...]])
    whole[...] = dot(left, right, TN).astype(BF16)
    hand_out(offsets, kept_ref.shape[1], whole, kept_ref, sends)


def norm_one_back(halves, gain_ref, one_ref, low_ref, sums_ref):
    totals = []
    for part, (own_ref, got_ref, two_ref, n_ref, scale_ref) in enumerate(halves):
        rows = own_ref.shape[0]
        mine = slice(part * rows, (part + 1) * rows)
        e = own_ref[...].astype(F32) + got_ref[...].astype(F32) + two_ref[...]
        n = n_ref[...]
        grad = norm_back(e, n, scale_ref[:, 0:1], gain_ref[0:1, :])
        one_ref[mine] = grad
        low_ref[mine] = grad.astype(BF16)
        totals.append([jnp.sum(values, axis=0, keepdims=True) for values in (e * n, e, grad)])
    for row in range(3):
        sums_ref[row : row + 1, :] = totals[0][row] + totals[1][row]


def attention_back_kernel(heads, scale, *refs):
    halves, refs = (refs[:5], refs[5:10]), refs[10:]
    (gain_ref, whole_ref, qkv_in, prob_in, one_ref, low_ref, norm_sums_ref, grads_ref, sums_ref,
     given, qkv_ref, prob_ref, sems) = refs
    copies = [pltpu.make_async_copy(qkv_in, qkv_ref, sems.at[heads])]
    for h in range(heads):
        copies.append(pltpu.make_async_copy(prob_in.at[h], prob_ref.at[h], sems.at[h]))
    for copy in copies:
        copy.start()
    norm_one_back(halves, gain_ref, one_ref, low_ref, norm_sums_ref)
    given[...] = dot(low_ref[...], whole_ref[3]).astype(BF16)
    rows = given.shape[0]
    lane = lax.broadcasted_iota(jnp.int32, (rows, PAIR), 1)
    copies[0].wait()
    for pair in range(heads // 2):
        columns = slice(pair * PAIR, (pair + 1) * PAIR)
        q = qkv_ref[0, :, columns]
        d = given[:, columns]
        keys = apart(qkv_ref[1, :, columns])
        d_probs = dot(apart(qkv_ref[2, :, columns]), d, NT)
        probs, scores = [], []
        for side in range(2):
            copies[1 + 2 * pair + side].wait()
            prob = prob_ref[2 * pair + side]
            wide = prob.astype(F32)
            d_prob = d_probs[side * rows : (side + 1) * rows]
            center = jnp.sum(d_prob * wide, axis=0, keepdims=True)
            probs.append(prob)
            scores.append((wide * (d_prob - center)).astype(BF16))
        score = jnp.concatenate(scores)
        d_keys = dot(score, q)
        d_values = dot(jnp.concatenate(probs), d)
        d_queries = dot(keys, score, TN).T
        for s, both in enumerate(
            (
                d_queries * scale,
                jnp.where(lane < HEAD, d_keys[:rows], d_keys[rows:]) * scale,
                jnp.where(lane < HEAD, d_values[:rows], d_values[rows:]),
            )
        ):
            both = both.astype(BF16)
            grads_ref[s, :, columns] = both
            if s != 1:
                sums_ref[s // 2 : s // 2 + 1, columns] = jnp.sum(both.astype(F32), axis=0, keepdims=True)


def input_grad_kernel(whole_ref, grads_ref, out_ref):
    total = dot(grads_ref[0], whole_ref[0], NT)
    total = total + dot(grads_ref[1], whole_ref[1], NT)
    total = total + dot(grads_ref[2], whole_ref[2], NT)
    out_ref[...] = total.astype(BF16)


def mixer_grad_kernel(offsets, vectors, tokens_ref, grads_ref, low_ref, attended_ref, *refs):
    vector_refs, (kept_ref, *sends, rider_ref, whole, packed) = refs[:vectors], refs[vectors:]
    pack(vector_refs, packed)
    coded, rider_ref[...] = ride(packed[...])
    sends[0][8 // len(sends) * 4] = coded
    for mat in range(4):
        if mat < 3:
            whole[...] = dot(tokens_ref[...], grads_ref[mat], TN).astype(BF16)
        else:
            whole[...] = dot(low_ref[...], attended_ref[...], TN).astype(BF16)
        hand_out(offsets, kept_ref.shape[1], whole, kept_ref, sends, 4, mat)


def add_kernel(cuts, *refs):
    gots, (own_ref, rest_ref, out_ref) = refs[:cuts], refs[cuts:]
    out_ref[...] = own_ref[...].astype(F32) + joined(gots) + rest_ref[...]


def joined(refs):
    parts = [ref[...].astype(F32) for ref in refs]
    return jnp.concatenate(parts) if len(parts) > 1 else parts[0]


def plain_grad_kernel(left_ref, right_ref, out_ref):
    out_ref[...] = dot(left_ref[...], right_ref[...], TN)


def shards(
    dp,
    tokens,
    project_weight,
    project_bias,
    output_weight,
    output_bias,
    expand_weight,
    expand_bias,
    shrink_weight,
    norm_gain,
    norm_shift,
    doc_lengths,
    cluster_perm,
    masked,
    out_grad,
):
    rows, width = tokens.shape
    piece_rows, _, columns = project_weight.shape
    units = expand_weight.shape[1]
    heads = columns // HEAD
    scale = HEAD**-0.5
    in_pieces = dp == 16 and piece_rows % 16 == 0 and piece_rows == 48 and columns == 384
    plan = Plan()
    note, hold = plan.note, plan.hold

    def whole(*shape):
        return pltpu.VMEM(shape, BF16)

    def sems(count):
        return pltpu.SemaphoreType.DMA((count,))

    (mixer_shard,) = call(
        bundle_kernel,
        [((4, piece_rows, columns), BF16)],
        [Away(project_weight.transpose(1, 0, 2)), Away(output_weight.T)],
        "bundle",
        scratch=[sems(2)],
    )
    m = {0: mixer_shard}
    if in_pieces:
        for o, source, step in ((8, 0, 8), (2, 0, 2), (4, 0, 4)):
            m[o] = plan.swap(f"m{o}", m[source], step)
    admit, feed_shard = call(
        functools.partial(prepare_kernel, heads, doc_lengths.shape[1]),
        [((heads, rows, rows), BF16), ((2, piece_rows, units), BF16)],
        [hold("prepare", doc_lengths), cluster_perm.transpose(1, 0, 2), Away(expand_weight), Away(shrink_weight.T)],
        "prepare",
        scratch=[sems(2)],
    )
    note("prepare", admit)
    f = {0: feed_shard}
    if in_pieces:
        for key in ORDER_BEFORE:
            pieces = m if key[0] == "m" else f
            o, source, step = hop(key)
            pieces[o] = plan.swap(key, pieces[source], step)
        mixer_all = [m[o] for o in range(dp)]
    else:
        mixer_all = [lax.all_gather(mixer_shard, "dp", axis=1, tiled=True)]
        feed_all = [lax.all_gather(feed_shard, "dp", axis=1, tiled=True)]
    count = len(mixer_all)

    qkv, prob, attended, attention_own, mixer = call(
        functools.partial(attention_kernel, count, heads, scale),
        [
            ((3, rows, columns), BF16, "hbm"),
            ((heads, rows, rows), BF16, "hbm"),
            ((rows, columns), BF16),
            ((rows, width), BF16),
            ((4, width, columns), BF16),
        ],
        [*mixer_all, Away(tokens), Away(project_bias), hold("attention", admit)],
        "attention",
        scratch=[
            whole(3, rows, columns), whole(heads, rows, rows), whole(rows, width),
            pltpu.VMEM((2, columns), F32), sems(5 + heads),
        ],
    )
    note("attention", mixer)
    attention_got = [plan.other("y1", attention_own, 0)]
    attention_got.append(plan.other("y1", attention_own, 1))
    attention_got = [x for x in attention_got if x is not None]
    if in_pieces:
        for key in ORDER_AFTER:
            o, source, step = hop(key)
            f[o] = plan.swap(key, f[source], step)
        feed_all = [f[o] for o in range(dp)]
    half_rows = rows // 2
    forward, feed = [], None
    for part in range(2):
        got = attention_got[part] if len(attention_got) == 2 else attention_got[0]
        outs = [
            ((half_rows, width), F32),
            ((half_rows, PAIR), F32),
            ((half_rows, width), BF16),
            ((half_rows, units), BF16),
            ((half_rows, units), BF16),
            ((half_rows, width), BF16),
        ]
        bias = hold(f"feed{part}", output_bias)
        weights = [feed] if part else feed_all
        result = call(
            functools.partial(feed_kernel, count, part, not part),
            outs if part else [*outs, ((2, width, units), BF16)],
            [*weights, got, tokens, attention_own, bias, norm_gain, norm_shift, expand_bias[None, :]],
            f"feed_forward_{part}",
        )
        if not part:
            *result, feed = result
        note(f"feed{part}", result[5])
        forward.append((*result, plan.other(f"y2{part}", result[5])))
    back, seed = [], masked.astype(F32)[:, None]
    for part in range(2):
        n_one, scale_one, first_low, active_low, slope, feed_own, feed_got = forward[part]
        result = call(
            functools.partial(feed_back_kernel, part),
            [
                ((rows, width), BF16, "free") if part else ((half_rows, width), BF16),
                ((half_rows, width), F32),
                ((half_rows, width), BF16),
                ((half_rows, units), BF16),
                ((half_rows, width), BF16),
                ((3, width), F32),
                ((1, units), F32),
            ],
            [
                feed, n_one, feed_own, feed_got, hold(f"feed_back{part}", output_bias), norm_gain, norm_shift,
                out_grad, seed, slope, *((back[0][0], *back[0][5:7]) if part else ()),
            ],
            f"feed_backward_{part}",
        )
        note(f"feed_back{part}", result[4])
        back.append((*result, plan.other(f"y3{part}", result[4])))
    layer_out, sums_two, inner_sum = back[1][0], back[1][5], back[1][6]

    def plain_grad(left, right, name):
        (grad,) = call(plain_grad_kernel, [((width, right.shape[1]), F32, "free")], [left, right], name)
        return lax.psum_scatter(grad, "dp", scatter_dimension=0, tiled=True)

    grads_of = (
        ([x[2] for x in back], [x[3] for x in forward]),
        ([x[2] for x in forward], [x[3] for x in back]),
    )

    def weight_grad(left, right, name, steps, split):
        wide = right[0].shape[1]
        parts = split[0]
        outs = [((8, piece_rows, wide), BF16)] + [((8 // parts, piece_rows, wide), BF16)] * parts
        kept, *sends = call(
            functools.partial(weight_grad_kernel, offsets_of(steps)),
            outs,
            [*left, right[0], hold(name, right[1])],
            name,
            scratch=[whole(width, wide)],
        )
        note(name, kept)
        return Reduction(plan, name, kept, sends, steps, split[1:])

    if in_pieces:
        shrink = weight_grad(*grads_of[0], "s", *SHRINK_STEPS)
        expand = weight_grad(*grads_of[1], "e", *EXPAND_STEPS)
        shrink.send()
        expand.send()
        shrink.forward()
        shrink.send()
        expand.forward()
        expand.send()
    residual_one, attention_low, sums_one, project_low, project_sums = call(
        functools.partial(attention_back_kernel, heads, scale),
        [
            ((rows, width), F32),
            ((rows, width), BF16),
            ((3, width), F32),
            ((3, rows, columns), BF16),
            ((2, columns), F32),
        ],
        [
            *(x for p in range(2) for x in (back[p][4], back[p][7], back[p][1], *forward[p][:2])),
            hold("back", norm_gain), mixer, Away(qkv), Away(prob),
        ],
        "attention_backward",
        scratch=[
            whole(rows, columns), whole(3, rows, columns), whole(heads, rows, rows), sems(heads + 1),
        ],
    )
    note("back", project_low)
    vectors = [sums_one, sums_two, inner_sum, project_sums]
    shapes = [v.shape for v in vectors]
    order = [[(2, 0), (3, 0), (1, 0)], [(2, 1), (3, 1), (1, 1)], [(4, 0)], [(0, 0), (0, 1)]]
    vector_outs = [
        ((2, columns), F32, "free"),
        ((2, width), F32, "free"),
        ((2, width), F32, "free"),
        ((2, width), F32, "free"),
        ((units // PAIR, PAIR), F32, "free"),
    ]

    def input_grad():
        (own,) = call(
            input_grad_kernel,
            [((rows, width), BF16)],
            [mixer, hold("input", project_low)],
            "input_grad",
        )
        note("input", own)
        gots = [plan.other("y4", own, 0)]
        gots.append(plan.other("y4", own, 1))
        gots = [x for x in gots if x is not None]
        (result,) = call(
            functools.partial(add_kernel, len(gots)),
            [((rows, width), F32, "free")],
            [*gots, own, hold("tokens", residual_one)],
            "tokens_grad",
        )
        return note("tokens", result)

    if in_pieces:
        steps, split = MIXER_STEPS
        parts = split[0]
        half = piece_rows // 2
        kept, *sends, rider = call(
            functools.partial(mixer_grad_kernel, offsets_of(steps), len(vectors)),
            [((32, piece_rows, columns), BF16)]
            + [((8 // parts * 4 + (i == 0), piece_rows, columns), BF16) for i in range(parts)]
            + [((half, columns), F32)],
            [tokens, hold("x", project_low), attention_low, attended, *vectors],
            "mixer_grad",
            scratch=[whole(width, columns), pltpu.VMEM((half, columns), F32)],
        )
        note("x", kept)
        mixed = Reduction(plan, "x", kept, sends, steps, split[1:], rider)
        parts_of = {"s": shrink, "e": expand, "x": mixed}
        block = (piece_rows, units)
        for key in ORDER_TAIL:
            if key == "input":
                tokens_grad = input_grad()
            elif key == "s_end":
                (shrink_part,) = shrink.finish(last_kernel, [(block, F32, "free")])
            elif key == "e_end":
                (expand_part,) = expand.finish(last_kernel, [(block, F32, "free")])
            elif key[1:] == "f":
                parts_of[key[0]].forward()
            else:
                parts_of[key[0]].send()
        project_part, output_part, *totals = mixed.finish(
            functools.partial(last_mixer_kernel, order, shapes),
            [((3, piece_rows, columns), F32, "free"), ((piece_rows, columns), F32, "free"), *vector_outs],
        )
    else:
        tokens_grad = input_grad()
        height = -(-sum(v.size for v in vectors) // PAIR // 8) * 8
        (packed,) = call(pack_kernel, [((height, PAIR), F32)], vectors, "pack")
        totals = call(
            functools.partial(unpack_kernel, order, shapes), vector_outs, [lax.psum(packed, "dp")], "unpack"
        )
        shrink_part, expand_part = (
            plain_grad(jnp.concatenate(left), jnp.concatenate(right), name)
            for (left, right), name in zip(grads_of, ("shrink_grad", "expand_grad"))
        )
        project_part = jnp.stack([plain_grad(tokens, project_low[s], "project_grad") for s in range(3)])
        output_part = plain_grad(attention_low, attended, "output_grad")
    project_total, output_total, gain_total, shift_total, inner_total = totals
    return (
        layer_out,
        tokens_grad,
        project_part.transpose(1, 0, 2),
        project_total,
        output_part.T,
        output_total,
        expand_part,
        inner_total.reshape(units),
        shrink_part.T,
        gain_total,
        shift_total,
    )


def solution(mesh):
    in_specs = (
        P("dp", None),
        P("dp", None, "tensor"),
        P(None, "tensor"),
        P("tensor", "dp"),
        P(),
        P("dp", "tensor"),
        P("tensor"),
        P("tensor", "dp"),
        P(),
        P(),
        P("dp", None),
        P("dp", "tensor", None),
        P("dp"),
        P("dp", None),
    )
    out_specs = (
        P("dp", None),
        P("dp", None),
        P("dp", None, "tensor"),
        P(None, "tensor"),
        P("tensor", "dp"),
        P(),
        P("dp", "tensor"),
        P("tensor"),
        P("tensor", "dp"),
        P(),
        P(),
    )
    body = functools.partial(shards, mesh.shape["dp"])
    return jax.shard_map(body, mesh=mesh, in_specs=in_specs, out_specs=out_specs, check_vma=False)
```

```python
import functools

import jax
import jax.numpy as jnp
from jax import lax
from jax.experimental import pallas as pl
from jax.experimental.pallas import tpu as pltpu
from jax.sharding import PartitionSpec as P

HEAD = 64
CLUSTER = 128
PAIR = 128
NORM_EPS = 1e-05
EXCLUDED = -1e30
VMEM_BYTES = 24 * 1024 * 1024
CUTS = {"y1": 192, "y4": 96}

HOPS = {o: (o, o & 12, 2) if o & 2 else (o, 0, o) for o in range(2, 16, 2)}
HOPS.update({o + 1: (o + 1, o, 1) for o in range(0, 16, 2)})
FAR = {"m": 8, "f": 8}
ORDER_BEFORE = (
    "m12", "m6", "m10", "m1", "m3", "m5", "m9", "f8", "f4", "m14", "m7", "f5",
    "m11", "m13", "m15", "f2",
)
ORDER_AFTER = (
    "f12", "f6", "f10", "f1", "f3", "f9", "f14", "f7", "f11", "f13", "f15",
)
SHRINK_STEPS = ((1, 4, 8, 2), (1, 1, 1, 1))
EXPAND_STEPS = ((1, 2, 4, 8), (1, 1, 1, 1))
MIXER_STEPS = ((1, 2, 4, 8), (4, 2, 2, 1))
ORDER_TAIL = (
    "x", "sf", "s", "ef", "e", "xf", "ef", "x", "input", "e", "sf", "s",
    "xf", "x", "s_end", "e_end", "xf", "x",
)
WAITS = {
    "e": ("m15",),
    "e1": ("y30",),
    "e2": ("f7",),
    "e4": ("feed_back0",),
    "e8": ("x2b", "y4a",),
    "e_end": ("x4a",),
    "e_to_2": ("s_to_4",),
    "f10": ("attention",),
    "f12": ("attention",),
    "f7": ("f4",),
    "f9": ("attention",),
    "m9": ("m8",),
    "tokens": ("x_to_2",),
    "x4a": ("x_to_4",),
    "x_to_2": ("s4", "e2",),
    "x_to_4": ("e4", "x1c",),
    "x_to_8": ("x2b",),
    "y21": ("feed0",),
    "y4b": ("input",),
}

F32 = jnp.float32
BF16 = jnp.bfloat16

NN = (((1,), (0,)), ((), ()))
NT = (((1,), (1,)), ((), ()))
TN = (((0,), (0,)), ((), ()))


def dot(a, b, dims=NN):
    return lax.dot_general(a, b, dims, preferred_element_type=F32)


def swap(array, axis, offset, size):
    return lax.ppermute(array, axis, [(i, i ^ offset) for i in range(size)])


def after(array, *earlier):
    return lax.optimization_barrier((array, *earlier))[0]


class Plan:
    def __init__(self):
        self.made = {}

    def hold(self, name, array):
        gates = [self.made[g] for g in WAITS.get(name, ()) if g in self.made]
        return after(array, *gates) if gates else array

    def note(self, name, array):
        self.made[name] = array
        return array

    def swap(self, name, array, offset):
        return self.note(name, swap(self.hold(name, array), "dp", offset, 16))

    def other(self, name, array, part=None):
        cut = CUTS.get(name, 0)
        if not cut:
            return self.note(name, other_half(self.hold(name, array))) if part != 1 else None
        rows = array[:cut] if part == 0 else array[cut:]
        name = name + "ab"[part]
        return self.note(name, other_half(self.hold(name, rows)))


def offsets_of(steps):
    offsets = [0]
    for step in reversed(steps):
        offsets = offsets + [o ^ step for o in offsets]
    return offsets


def hop(key):
    o, source, step = HOPS[int(key[1:])]
    if o == 12 and FAR[key[0]]:
        source, step = FAR[key[0]], 12 ^ FAR[key[0]]
    return o, source, step


class Reduction:
    def __init__(self, plan, name, kept, sends, steps, split, rider=None):
        self.plan, self.name, self.kept, self.sends = plan, name, kept, sends
        self.steps, self.split, self.rider = list(steps), list(split), rider
        self.arrived = []
        self.count = 8

    def send(self):
        step = self.steps.pop(0)
        count = self.count
        pieces = len(self.sends)
        per = count // pieces
        for i, array in enumerate(self.sends):
            name = f"{self.name}{step}" + ("abcd"[i] if pieces > 1 else "")
            got = self.plan.swap(name, array, step)
            self.arrived.append((count - (i + 1) * per, per, got, self.rider is not None and i == 0))
        self.step = step
        self.count = count // 2

    def forward(self):
        count = self.count
        parts = min(self.split.pop(0), count)
        per = count // parts
        ranges = [(2 * count - (i + 1) * per, per) for i in range(parts)]
        needed = [a for a in self.arrived if a[0] + a[1] > count]
        name = f"{self.name}_to_{self.steps[0]}"
        self.sends = self.total(name, ranges, needed)

    def total(self, name, ranges, needed):
        mats = 1 if self.rider is None else 4
        block = self.kept.shape[1:]
        outs = []
        for i, (_, blocks) in enumerate(ranges):
            extra = 1 if self.rider is not None and i == 0 else 0
            outs.append(((blocks * mats + extra, *block), BF16))
        ins = [self.kept, *(a[2] for a in needed)]
        if self.rider is not None:
            outs.append((self.rider.shape, F32))
            ins.append(self.rider)
        ins[1] = self.plan.hold(name, ins[1])
        body = functools.partial(forward_kernel, mats, tuple(ranges), tuple((a[0], a[1], a[3]) for a in needed))
        result = list(call(body, outs, ins, name))
        self.plan.note(name, result[0])
        for i, a in enumerate(self.arrived):
            self.arrived[i] = (a[0], a[1], a[2], False)
        if self.rider is not None:
            self.rider = result.pop()
        return result

    def finish(self, body, outs):
        name = f"{self.name}_end"
        ins = [self.kept, *(a[2] for a in self.arrived)]
        if self.rider is not None:
            ins.append(self.rider)
        ins[1] = self.plan.hold(name, ins[1])
        mats = 1 if self.rider is None else 4
        body = functools.partial(body, mats, tuple((a[0], a[1], a[3]) for a in self.arrived))
        result = call(body, outs, ins, name)
        self.plan.note(name, result[0])
        return result


def ride(vector):
    high = vector.astype(BF16)
    low = (vector - high.astype(F32)).astype(BF16)
    return jnp.concatenate([high, low]), high.astype(F32) + low.astype(F32)


def unride(block):
    half = block.shape[0] // 2
    return block[:half].astype(F32) + block[half:].astype(F32)


def sum_blocks(mats, first, count, kept, gots, places):
    total = kept[first * mats : (first + count) * mats].astype(F32)
    for ref, (start, blocks, _) in zip(gots, places):
        low, high = max(start, first), min(start + blocks, first + count)
        if low < high:
            part = ref[(low - start) * mats : (high - start) * mats].astype(F32)
            pieces = [total[: (low - first) * mats]] if low > first else []
            pieces.append(total[(low - first) * mats : (high - first) * mats] + part)
            if high < first + count:
                pieces.append(total[(high - first) * mats :])
            total = jnp.concatenate(pieces) if len(pieces) > 1 else pieces[0]
    return total


def next_vector(mats, gots, places, rider_ref):
    vector = rider_ref[...]
    for ref, (_, blocks, rides) in zip(gots, places):
        if rides:
            vector = vector + unride(ref[blocks * mats])
    return vector


def forward_kernel(mats, ranges, places, kept, *refs):
    gots, refs = refs[: len(places)], refs[len(places) :]
    if mats > 1:
        rider_ref, outs, rider_out = refs[0], refs[1:-1], refs[-1]
        coded, rider_out[...] = ride(next_vector(mats, gots, places, rider_ref))
        outs[0][ranges[0][1] * mats] = coded
    else:
        outs = refs
    for out, (first, count) in zip(outs, ranges):
        out[: count * mats] = sum_blocks(mats, first, count, kept, gots, places).astype(BF16)


def last_kernel(mats, places, kept, *refs):
    gots, out_ref = refs[:-1], refs[-1]
    out_ref[...] = sum_blocks(mats, 0, 1, kept, gots, places)[0]


def last_mixer_kernel(order, shapes, mats, places, kept, *refs):
    gots, rider_ref, outs = refs[: len(places)], refs[len(places)], refs[len(places) + 1 :]
    total = sum_blocks(mats, 0, 1, kept, gots, places)
    outs[0][...] = total[:-1]
    outs[1][...] = total[-1]
    vector = next_vector(mats, gots, places, rider_ref)
    unpack(order, shapes, vector, outs[2:])


def rows_of(shapes, wide):
    places = []
    for i, (height, width) in enumerate(shapes):
        places += [(i, r, slice(c, c + wide)) for r in range(height) for c in range(0, width, wide)]
    return places


def pack(refs, out_ref):
    wide = out_ref.shape[1]
    out_ref[...] = jnp.zeros(out_ref.shape, F32)
    for k, (i, r, columns) in enumerate(rows_of([ref.shape for ref in refs], wide)):
        out_ref[k : k + 1, :] = refs[i][r : r + 1, columns]


def unpack(order, shapes, vector, outs):
    wide = vector.shape[1]
    for k, (i, r, columns) in enumerate(rows_of(shapes, wide)):
        out, row = order[i][r]
        part = vector[k : k + 1, :]
        if outs[out].shape[1] == PAIR:
            for j in range(wide // PAIR):
                at = columns.start // PAIR + j
                outs[out][at : at + 1, :] = part[:, j * PAIR : (j + 1) * PAIR]
        else:
            outs[out][row : row + 1, columns] = part


def pack_kernel(*refs):
    pack(refs[:-1], refs[-1])


def unpack_kernel(order, shapes, in_ref, *outs):
    unpack(order, shapes, in_ref[...], outs)


def other_half(array):
    return lax.ppermute(array, "tensor", [(0, 1), (1, 0)])


def call(body, outs, ins, name, scratch=()):
    kinds = [o[2] if len(o) > 2 else "vmem" for o in outs]
    make = {"vmem": pltpu.VMEM, "hbm": pltpu.HBM, "free": jax.ShapeDtypeStruct}
    in_specs, values = [], []
    for x in ins:
        away = isinstance(x, Away)
        in_specs.append(pl.BlockSpec(memory_space=pl.ANY if away else pltpu.VMEM))
        values.append(pltpu.with_memory_space_constraint(x.array, pltpu.HBM) if away else x)
    return pl.pallas_call(
        body,
        out_shape=tuple(make[k](o[0], o[1]) for o, k in zip(outs, kinds)),
        in_specs=in_specs,
        out_specs=tuple(
            pl.BlockSpec(memory_space=pl.ANY if k == "hbm" else pltpu.VMEM) for k in kinds
        ),
        scratch_shapes=list(scratch),
        compiler_params=pltpu.CompilerParams(vmem_limit_bytes=VMEM_BYTES),
        name=name,
    )(*values)


class Away:
    def __init__(self, array):
        self.array = array


def assemble(pieces, whole):
    count = len(pieces)
    me = lax.axis_index("dp") if count > 1 else 0
    for o, piece in enumerate(pieces):
        rows = piece.shape[-2]
        start = pl.multiple_of((me ^ o) * rows, 16) if count > 1 else 0
        if len(piece.shape) == 3:
            whole[:, pl.ds(start, rows), :] = piece[...]
        else:
            whole[pl.ds(start, rows), :] = piece[...]


def norm_rows(v):
    center = jnp.mean(v, axis=-1, keepdims=True)
    offset = v - center
    spread = jnp.mean(offset * offset, axis=-1, keepdims=True)
    scale = lax.rsqrt(spread + NORM_EPS)
    return offset * scale, scale


def norm_back(e, n, scale, gain):
    ea = e * gain
    return scale * (
        ea
        - jnp.mean(ea, axis=-1, keepdims=True)
        - n * jnp.mean(ea * n, axis=-1, keepdims=True)
    )


def bundle_kernel(project_ref, output_ref, out_ref, sems):
    one = pltpu.make_async_copy(project_ref, out_ref.at[pl.ds(0, 3)], sems.at[0])
    two = pltpu.make_async_copy(output_ref, out_ref.at[3], sems.at[1])
    one.start()
    two.start()
    one.wait()
    two.wait()


def prepare_kernel(heads, docs, lengths_ref, perm_ref, expand_ref, shrink_ref, bias_ref, feed_ref, sems):
    one = pltpu.make_async_copy(expand_ref, feed_ref.at[0], sems.at[0])
    two = pltpu.make_async_copy(shrink_ref, feed_ref.at[1], sems.at[1])
    one.start()
    two.start()
    rows = bias_ref.shape[1]
    spot = lax.broadcasted_iota(jnp.int32, (rows, PAIR), 0)
    lane = lax.broadcasted_iota(jnp.int32, (rows, PAIR), 1)
    doc = jnp.zeros((rows, PAIR), jnp.int32)
    bound = jnp.int32(0)
    for k in range(docs):
        bound = bound + lengths_ref[0, k]
        doc = doc + (spot >= bound).astype(jnp.int32)
    doc_hot = (lane == doc + PAIR // 2).astype(F32)
    cluster_hot = (lane == spot // CLUSTER).astype(BF16)
    place = lax.broadcasted_iota(jnp.int32, (rows, rows), 0)
    for h in range(heads):
        here = (place == perm_ref[h]).astype(BF16)
        key = (dot(here, cluster_hot) + doc_hot).astype(BF16)
        same = dot(key, key, NT)
        bias_ref[h] = jnp.where(same > 1.5, 0.0, EXCLUDED).astype(BF16)
    one.wait()
    two.wait()


def apart(pair):
    lane = lax.broadcasted_iota(jnp.int32, pair.shape, 1)
    zeros = jnp.zeros_like(pair)
    return jnp.concatenate([jnp.where(lane < HEAD, pair, zeros), jnp.where(lane < HEAD, zeros, pair)])


def attention_kernel(count, heads, scale, *refs):
    pieces, refs = refs[:count], refs[count:]
    (tokens_in, bias_in, admit_ref, qkv_out, prob_out, attended_ref, out_ref, whole,
     qkv_ref, prob_ref, tokens_ref, bias_ref, sems) = refs
    last = sems.shape[0]
    copies = [
        pltpu.make_async_copy(tokens_in, tokens_ref, sems.at[last - 2]),
        pltpu.make_async_copy(bias_in, bias_ref, sems.at[last - 1]),
    ]
    for copy in copies:
        copy.start()
    assemble(pieces, whole)
    for copy in copies:
        copy.wait()
    tokens = tokens_ref[...]
    rows = tokens.shape[0]
    copies = []

    def away(source, target):
        copies.append(pltpu.make_async_copy(source, target, sems.at[len(copies)]))
        copies[-1].start()

    for s in range(3):
        part = dot(tokens, whole[s])
        if s == 0:
            part = part + bias_ref[0:1, :]
        if s == 2:
            part = part + bias_ref[1:2, :]
        qkv_ref[s] = part.astype(BF16)
        away(qkv_ref.at[s], qkv_out.at[s])
    for pair in range(heads // 2):
        columns = slice(pair * PAIR, (pair + 1) * PAIR)
        keys = apart(qkv_ref[1, :, columns])
        scores = dot(keys, qkv_ref[0, :, columns] * scale, NT)
        probs = []
        for side in range(2):
            h = 2 * pair + side
            terms = scores[side * rows : (side + 1) * rows] + admit_ref[h].astype(F32)
            terms = jnp.exp(terms - jnp.max(terms, axis=0, keepdims=True))
            prob = (terms * (1.0 / jnp.sum(terms, axis=0, keepdims=True))).astype(BF16)
            prob_ref[h] = prob
            away(prob_ref.at[h], prob_out.at[h])
            probs.append(prob)
        mixed = dot(apart(qkv_ref[2, :, columns]), jnp.concatenate(probs), TN)
        attended_ref[:, columns] = mixed.T.astype(BF16)
    out_ref[...] = dot(attended_ref[...], whole[3], NT).astype(BF16)
    for copy in copies:
        copy.wait()


def feed_kernel(count, part, gather, *refs):
    if gather:
        pieces, refs = refs[:count], refs[count:]
        whole, refs = refs[-1], refs[:-1]
        assemble(pieces, whole)
    else:
        whole, refs = refs[0], refs[1:]
    (got_ref, tokens_ref, own_ref, out_bias_ref, gain_ref, shift_ref, bias_ref,
     n_ref, scale_ref, low_ref, active_ref, slope_ref, out_ref) = refs
    rows = n_ref.shape[0]
    mine = slice(part * rows, (part + 1) * rows)
    got = got_ref[...] if got_ref.shape[0] == rows else got_ref[mine]
    attention = own_ref[mine].astype(F32) + got.astype(F32) + out_bias_ref[0:1, :]
    n, scale = norm_rows(tokens_ref[mine].astype(F32) + attention)
    n_ref[...] = n
    scale_ref[...] = jnp.broadcast_to(scale, scale_ref.shape)
    low_ref[...] = (n * gain_ref[0:1, :] + shift_ref[0:1, :]).astype(BF16)
    units = whole.shape[2]
    step = 512
    for start in range(0, units, step):
        columns = slice(start, start + step)
        pre = dot(low_ref[...], whole[0, :, columns]) + bias_ref[:, columns]
        half = 0.5 * (1.0 + lax.erf(pre * (2.0**-0.5)))
        active_ref[:, columns] = (pre * half).astype(BF16)
        bell = jnp.exp(-0.5 * pre * pre) * 0.3989422804014327
        slope_ref[:, columns] = (half + pre * bell).astype(BF16)
    out_ref[...] = dot(active_ref[...], whole[1], NT).astype(BF16)


def feed_back_kernel(part, *refs):
    (whole, n_ref, own_ref, got_ref, out_bias_ref, gain_ref, shift_ref, seed_ref, masked_ref, slope_ref,
     *refs) = refs
    if part:
        layer_first, sums_first, inner_first, *refs = refs
    layer_ref, two_ref, low_ref, inner_ref, first_ref, sums_ref, inner_sum_ref = refs
    rows = n_ref.shape[0]
    mine = slice(part * rows, (part + 1) * rows)
    first = n_ref[...] * gain_ref[0:1, :] + shift_ref[0:1, :]
    feed = own_ref[...].astype(F32) + got_ref[...].astype(F32) + out_bias_ref[1:2, :]
    n, scale = norm_rows(first + feed)
    gain = gain_ref[1:2, :]
    layer = (n * gain + shift_ref[1:2, :]).astype(BF16)
    if part:
        layer_ref[:rows] = layer_first[...]
        layer_ref[mine] = layer
    else:
        layer_ref[...] = layer
    e = seed_ref[mine].astype(F32) * masked_ref[mine]
    grad = norm_back(e, n, scale, gain)
    two_ref[...] = grad
    low_ref[...] = grad.astype(BF16)
    for row, values in enumerate((e * n, e, grad)):
        total = jnp.sum(values, axis=0, keepdims=True)
        sums_ref[row : row + 1, :] = total + sums_first[row : row + 1, :] if part else total
    units = whole.shape[2]
    step = 512
    for start in range(0, units, step):
        columns = slice(start, start + step)
        slope = slope_ref[:, columns].astype(F32)
        inner = (dot(low_ref[...], whole[1, :, columns]) * slope).astype(BF16)
        inner_ref[:, columns] = inner
        total = jnp.sum(inner.astype(F32), axis=0, keepdims=True)
        inner_sum_ref[:, columns] = total + inner_first[:, columns] if part else total
    first_ref[...] = dot(inner_ref[...], whole[0], NT).astype(BF16)


def hand_out(offsets, rows, whole, kept_ref, sends, mats=1, mat=0):
    me = lax.axis_index("dp")
    per = 8 // len(sends)
    for k, offset in enumerate(offsets):
        start = pl.multiple_of((me ^ offset) * rows, 16)
        block = whole[pl.ds(start, rows), :]
        if k < 8:
            kept_ref[k * mats + mat] = block
        else:
            part = len(sends) - 1 - (k - 8) // per
            sends[part][(k - 8) % per * mats + mat] = block


def weight_grad_kernel(offsets, left_a, left_b, right_a, right_b, kept_ref, *refs):
    sends, whole = refs[:-1], refs[-1]
    left = jnp.concatenate([left_a[...], left_b[...]])
    right = jnp.concatenate([right_a[...], right_b[...]])
    whole[...] = dot(left, right, TN).astype(BF16)
    hand_out(offsets, kept_ref.shape[1], whole, kept_ref, sends)


def norm_one_back(halves, gain_ref, one_ref, low_ref, sums_ref):
    totals = []
    for part, (own_ref, got_ref, two_ref, n_ref, scale_ref) in enumerate(halves):
        rows = own_ref.shape[0]
        mine = slice(part * rows, (part + 1) * rows)
        e = own_ref[...].astype(F32) + got_ref[...].astype(F32) + two_ref[...]
        n = n_ref[...]
        grad = norm_back(e, n, scale_ref[:, 0:1], gain_ref[0:1, :])
        one_ref[mine] = grad
        low_ref[mine] = grad.astype(BF16)
        totals.append([jnp.sum(values, axis=0, keepdims=True) for values in (e * n, e, grad)])
    for row in range(3):
        sums_ref[row : row + 1, :] = totals[0][row] + totals[1][row]


def attention_back_kernel(heads, scale, *refs):
    halves, refs = (refs[:5], refs[5:10]), refs[10:]
    (gain_ref, whole_ref, qkv_in, prob_in, one_ref, low_ref, norm_sums_ref, grads_ref, sums_ref,
     given, qkv_ref, prob_ref, sems) = refs
    copies = [pltpu.make_async_copy(qkv_in, qkv_ref, sems.at[heads])]
    for h in range(heads):
        copies.append(pltpu.make_async_copy(prob_in.at[h], prob_ref.at[h], sems.at[h]))
    for copy in copies:
        copy.start()
    norm_one_back(halves, gain_ref, one_ref, low_ref, norm_sums_ref)
    given[...] = dot(low_ref[...], whole_ref[3]).astype(BF16)
    rows = given.shape[0]
    lane = lax.broadcasted_iota(jnp.int32, (rows, PAIR), 1)
    copies[0].wait()
    for pair in range(heads // 2):
        columns = slice(pair * PAIR, (pair + 1) * PAIR)
        q = qkv_ref[0, :, columns]
        d = given[:, columns]
        keys = apart(qkv_ref[1, :, columns])
        d_probs = dot(apart(qkv_ref[2, :, columns]), d, NT)
        probs, scores = [], []
        for side in range(2):
            copies[1 + 2 * pair + side].wait()
            prob = prob_ref[2 * pair + side]
            wide = prob.astype(F32)
            d_prob = d_probs[side * rows : (side + 1) * rows]
            center = jnp.sum(d_prob * wide, axis=0, keepdims=True)
            probs.append(prob)
            scores.append((wide * (d_prob - center)).astype(BF16))
        score = jnp.concatenate(scores)
        d_keys = dot(score, q)
        d_values = dot(jnp.concatenate(probs), d)
        d_queries = dot(keys, score, TN).T
        for s, both in enumerate(
            (
                d_queries * scale,
                jnp.where(lane < HEAD, d_keys[:rows], d_keys[rows:]) * scale,
                jnp.where(lane < HEAD, d_values[:rows], d_values[rows:]),
            )
        ):
            both = both.astype(BF16)
            grads_ref[s, :, columns] = both
            if s != 1:
                sums_ref[s // 2 : s // 2 + 1, columns] = jnp.sum(both.astype(F32), axis=0, keepdims=True)


def input_grad_kernel(whole_ref, grads_ref, out_ref):
    total = dot(grads_ref[0], whole_ref[0], NT)
    total = total + dot(grads_ref[1], whole_ref[1], NT)
    total = total + dot(grads_ref[2], whole_ref[2], NT)
    out_ref[...] = total.astype(BF16)


def mixer_grad_kernel(offsets, vectors, tokens_ref, grads_ref, low_ref, attended_ref, *refs):
    vector_refs, (kept_ref, *sends, rider_ref, whole, packed) = refs[:vectors], refs[vectors:]
    pack(vector_refs, packed)
    coded, rider_ref[...] = ride(packed[...])
    sends[0][8 // len(sends) * 4] = coded
    for mat in range(4):
        if mat < 3:
            whole[...] = dot(tokens_ref[...], grads_ref[mat], TN).astype(BF16)
        else:
            whole[...] = dot(low_ref[...], attended_ref[...], TN).astype(BF16)
        hand_out(offsets, kept_ref.shape[1], whole, kept_ref, sends, 4, mat)


def add_kernel(cuts, *refs):
    gots, (own_ref, rest_ref, out_ref) = refs[:cuts], refs[cuts:]
    out_ref[...] = own_ref[...].astype(F32) + joined(gots) + rest_ref[...]


def joined(refs):
    parts = [ref[...].astype(F32) for ref in refs]
    return jnp.concatenate(parts) if len(parts) > 1 else parts[0]


def plain_grad_kernel(left_ref, right_ref, out_ref):
    out_ref[...] = dot(left_ref[...], right_ref[...], TN)


def shards(
    dp,
    tokens,
    project_weight,
    project_bias,
    output_weight,
    output_bias,
    expand_weight,
    expand_bias,
    shrink_weight,
    norm_gain,
    norm_shift,
    doc_lengths,
    cluster_perm,
    masked,
    out_grad,
):
    rows, width = tokens.shape
    piece_rows, _, columns = project_weight.shape
    units = expand_weight.shape[1]
    heads = columns // HEAD
    scale = HEAD**-0.5
    in_pieces = dp == 16 and piece_rows % 16 == 0 and piece_rows == 48 and columns == 384
    plan = Plan()
    note, hold = plan.note, plan.hold

    def whole(*shape):
        return pltpu.VMEM(shape, BF16)

    def sems(count):
        return pltpu.SemaphoreType.DMA((count,))

    (mixer_shard,) = call(
        bundle_kernel,
        [((4, piece_rows, columns), BF16)],
        [Away(project_weight.transpose(1, 0, 2)), Away(output_weight.T)],
        "bundle",
        scratch=[sems(2)],
    )
    m = {0: mixer_shard}
    if in_pieces:
        for o, source, step in ((8, 0, 8), (2, 0, 2), (4, 0, 4)):
            m[o] = plan.swap(f"m{o}", m[source], step)
    admit, feed_shard = call(
        functools.partial(prepare_kernel, heads, doc_lengths.shape[1]),
        [((heads, rows, rows), BF16), ((2, piece_rows, units), BF16)],
        [hold("prepare", doc_lengths), cluster_perm.transpose(1, 0, 2), Away(expand_weight), Away(shrink_weight.T)],
        "prepare",
        scratch=[sems(2)],
    )
    note("prepare", admit)
    f = {0: feed_shard}
    if in_pieces:
        for key in ORDER_BEFORE:
            pieces = m if key[0] == "m" else f
            o, source, step = hop(key)
            pieces[o] = plan.swap(key, pieces[source], step)
        mixer_all = [m[o] for o in range(dp)]
    else:
        mixer_all = [lax.all_gather(mixer_shard, "dp", axis=1, tiled=True)]
        feed_all = [lax.all_gather(feed_shard, "dp", axis=1, tiled=True)]
    count = len(mixer_all)

    qkv, prob, attended, attention_own, mixer = call(
        functools.partial(attention_kernel, count, heads, scale),
        [
            ((3, rows, columns), BF16, "hbm"),
            ((heads, rows, rows), BF16, "hbm"),
            ((rows, columns), BF16),
            ((rows, width), BF16),
            ((4, width, columns), BF16),
        ],
        [*mixer_all, Away(tokens), Away(project_bias), hold("attention", admit)],
        "attention",
        scratch=[
            whole(3, rows, columns), whole(heads, rows, rows), whole(rows, width),
            pltpu.VMEM((2, columns), F32), sems(5 + heads),
        ],
    )
    note("attention", mixer)
    attention_got = [plan.other("y1", attention_own, 0)]
    attention_got.append(plan.other("y1", attention_own, 1))
    attention_got = [x for x in attention_got if x is not None]
    if in_pieces:
        for key in ORDER_AFTER:
            o, source, step = hop(key)
            f[o] = plan.swap(key, f[source], step)
        feed_all = [f[o] for o in range(dp)]
    half_rows = rows // 2
    forward, feed = [], None
    for part in range(2):
        got = attention_got[part] if len(attention_got) == 2 else attention_got[0]
        outs = [
            ((half_rows, width), F32),
            ((half_rows, PAIR), F32),
            ((half_rows, width), BF16),
            ((half_rows, units), BF16),
            ((half_rows, units), BF16),
            ((half_rows, width), BF16),
        ]
        bias = hold(f"feed{part}", output_bias)
        weights = [feed] if part else feed_all
        result = call(
            functools.partial(feed_kernel, count, part, not part),
            outs if part else [*outs, ((2, width, units), BF16)],
            [*weights, got, tokens, attention_own, bias, norm_gain, norm_shift, expand_bias[None, :]],
            f"feed_forward_{part}",
        )
        if not part:
            *result, feed = result
        note(f"feed{part}", result[5])
        forward.append((*result, plan.other(f"y2{part}", result[5])))
    back, seed = [], masked.astype(F32)[:, None]
    for part in range(2):
        n_one, scale_one, first_low, active_low, slope, feed_own, feed_got = forward[part]
        result = call(
            functools.partial(feed_back_kernel, part),
            [
                ((rows, width), BF16, "free") if part else ((half_rows, width), BF16),
                ((half_rows, width), F32),
                ((half_rows, width), BF16),
                ((half_rows, units), BF16),
                ((half_rows, width), BF16),
                ((3, width), F32),
                ((1, units), F32),
            ],
            [
                feed, n_one, feed_own, feed_got, hold(f"feed_back{part}", output_bias), norm_gain, norm_shift,
                out_grad, seed, slope, *((back[0][0], *back[0][5:7]) if part else ()),
            ],
            f"feed_backward_{part}",
        )
        note(f"feed_back{part}", result[4])
        back.append((*result, plan.other(f"y3{part}", result[4])))
    layer_out, sums_two, inner_sum = back[1][0], back[1][5], back[1][6]

    def plain_grad(left, right, name):
        (grad,) = call(plain_grad_kernel, [((width, right.shape[1]), F32, "free")], [left, right], name)
        return lax.psum_scatter(grad, "dp", scatter_dimension=0, tiled=True)

    grads_of = (
        ([x[2] for x in back], [x[3] for x in forward]),
        ([x[2] for x in forward], [x[3] for x in back]),
    )

    def weight_grad(left, right, name, steps, split):
        wide = right[0].shape[1]
        parts = split[0]
        outs = [((8, piece_rows, wide), BF16)] + [((8 // parts, piece_rows, wide), BF16)] * parts
        kept, *sends = call(
            functools.partial(weight_grad_kernel, offsets_of(steps)),
            outs,
            [*left, right[0], hold(name, right[1])],
            name,
            scratch=[whole(width, wide)],
        )
        note(name, kept)
        return Reduction(plan, name, kept, sends, steps, split[1:])

    if in_pieces:
        shrink = weight_grad(*grads_of[0], "s", *SHRINK_STEPS)
        expand = weight_grad(*grads_of[1], "e", *EXPAND_STEPS)
        shrink.send()
        expand.send()
        shrink.forward()
        shrink.send()
        expand.forward()
        expand.send()
    residual_one, attention_low, sums_one, project_low, project_sums = call(
        functools.partial(attention_back_kernel, heads, scale),
        [
            ((rows, width), F32),
            ((rows, width), BF16),
            ((3, width), F32),
            ((3, rows, columns), BF16),
            ((2, columns), F32),
        ],
        [
            *(x for p in range(2) for x in (back[p][4], back[p][7], back[p][1], *forward[p][:2])),
            hold("back", norm_gain), mixer, Away(qkv), Away(prob),
        ],
        "attention_backward",
        scratch=[
            whole(rows, columns), whole(3, rows, columns), whole(heads, rows, rows), sems(heads + 1),
        ],
    )
    note("back", project_low)
    vectors = [sums_one, sums_two, inner_sum, project_sums]
    shapes = [v.shape for v in vectors]
    order = [[(2, 0), (3, 0), (1, 0)], [(2, 1), (3, 1), (1, 1)], [(4, 0)], [(0, 0), (0, 1)]]
    vector_outs = [
        ((2, columns), F32, "free"),
        ((2, width), F32, "free"),
        ((2, width), F32, "free"),
        ((2, width), F32, "free"),
        ((units // PAIR, PAIR), F32, "free"),
    ]

    def input_grad():
        (own,) = call(
            input_grad_kernel,
            [((rows, width), BF16)],
            [mixer, hold("input", project_low)],
            "input_grad",
        )
        note("input", own)
        gots = [plan.other("y4", own, 0)]
        gots.append(plan.other("y4", own, 1))
        gots = [x for x in gots if x is not None]
        (result,) = call(
            functools.partial(add_kernel, len(gots)),
            [((rows, width), F32, "free")],
            [*gots, own, hold("tokens", residual_one)],
            "tokens_grad",
        )
        return note("tokens", result)

    if in_pieces:
        steps, split = MIXER_STEPS
        parts = split[0]
        half = piece_rows // 2
        kept, *sends, rider = call(
            functools.partial(mixer_grad_kernel, offsets_of(steps), len(vectors)),
            [((32, piece_rows, columns), BF16)]
            + [((8 // parts * 4 + (i == 0), piece_rows, columns), BF16) for i in range(parts)]
            + [((half, columns), F32)],
            [tokens, hold("x", project_low), attention_low, attended, *vectors],
            "mixer_grad",
            scratch=[whole(width, columns), pltpu.VMEM((half, columns), F32)],
        )
        note("x", kept)
        mixed = Reduction(plan, "x", kept, sends, steps, split[1:], rider)
        parts_of = {"s": shrink, "e": expand, "x": mixed}
        block = (piece_rows, units)
        for key in ORDER_TAIL:
            if key == "input":
                tokens_grad = input_grad()
            elif key == "s_end":
                (shrink_part,) = shrink.finish(last_kernel, [(block, F32, "free")])
            elif key == "e_end":
                (expand_part,) = expand.finish(last_kernel, [(block, F32, "free")])
            elif key[1:] == "f":
                parts_of[key[0]].forward()
            else:
                parts_of[key[0]].send()
        project_part, output_part, *totals = mixed.finish(
            functools.partial(last_mixer_kernel, order, shapes),
            [((3, piece_rows, columns), F32, "free"), ((piece_rows, columns), F32, "free"), *vector_outs],
        )
    else:
        tokens_grad = input_grad()
        height = -(-sum(v.size for v in vectors) // PAIR // 8) * 8
        (packed,) = call(pack_kernel, [((height, PAIR), F32)], vectors, "pack")
        totals = call(
            functools.partial(unpack_kernel, order, shapes), vector_outs, [lax.psum(packed, "dp")], "unpack"
        )
        shrink_part, expand_part = (
            plain_grad(jnp.concatenate(left), jnp.concatenate(right), name)
            for (left, right), name in zip(grads_of, ("shrink_grad", "expand_grad"))
        )
        project_part = jnp.stack([plain_grad(tokens, project_low[s], "project_grad") for s in range(3)])
        output_part = plain_grad(attention_low, attended, "output_grad")
    project_total, output_total, gain_total, shift_total, inner_total = totals
    return (
        layer_out,
        tokens_grad,
        project_part.transpose(1, 0, 2),
        project_total,
        output_part.T,
        output_total,
        expand_part,
        inner_total.reshape(units),
        shrink_part.T,
        gain_total,
        shift_total,
    )


def solution(mesh):
    in_specs = (
        P("dp", None),
        P("dp", None, "tensor"),
        P(None, "tensor"),
        P("tensor", "dp"),
        P(),
        P("dp", "tensor"),
        P("tensor"),
        P("tensor", "dp"),
        P(),
        P(),
        P("dp", None),
        P("dp", "tensor", None),
        P("dp"),
        P("dp", None),
    )
    out_specs = (
        P("dp", None),
        P("dp", None),
        P("dp", None, "tensor"),
        P(None, "tensor"),
        P("tensor", "dp"),
        P(),
        P("dp", "tensor"),
        P("tensor"),
        P("tensor", "dp"),
        P(),
        P(),
    )
    body = functools.partial(shards, mesh.shape["dp"])
    return jax.shard_map(body, mesh=mesh, in_specs=in_specs, out_specs=out_specs, check_vma=False)
```
